128 devices in a mesh: dp: 32 (over y, z, x_hi), sp: 4 (over x_lo, core).
Axes of the slice: x: 4 (x_hi: 2, x_lo: 2; x = x_hi * 2 + x_lo), y: 4, z: 4, core: 2. Of those that a mesh axis runs over, the one named last changes fastest.
Arguments:
- queries: bfloat16 [16384, 2560], P(('dp', 'sp')), may hold values from -80 to 80
- key_rows: bfloat16 [16384, 2560], P(('dp', 'sp')), may hold values from -5 to 5
- value_rows: bfloat16 [16384, 2560], P(('dp', 'sp')), may hold values from -6 to 6
- cotangent: bfloat16 [16384, 2560], P(('dp', 'sp')), may hold values from -6 to 6
- lengths: int32 [32], replicated, may hold values from 1 to 512, 10240 in all
- sample_plan: int32 [32], replicated, may hold values from 0 to 31, each once
- guide_bins: int32 [32], replicated, may hold values from 0 to 7
- guide_table: float32 [8, 20], replicated, may hold values from 0.5 to 2
- block_source: int32 [16384], replicated, may hold values from 0 to 16383, as said below
Outputs:
- attn_out: bfloat16 [16384, 2560], P(('dp', 'sp'))
- grad_queries: bfloat16 [16384, 2560], P(('dp', 'sp'))
- grad_keys: bfloat16 [16384, 2560], P(('dp', 'sp'))
- grad_values: bfloat16 [16384, 2560], P(('dp', 'sp'))
The draws below stay inside these ranges and needn't reach their ends.
Inputs may be any that keep to these rules, and one draw needn't show every extreme that they name: `lengths`: the longest sample has exactly 512 tokens. `sample_plan`: every group takes exactly one sample. `block_source`: a permutation; the 128 row blocks of the group order that one device holds come one from each device's loader rows, and each device's 128 loader row blocks go one to each device.
All inputs are finite; a program needn't handle non-finite values.
Results may differ from the reference program's by a relative error of at most 0.009.
Values may be sent and summed in bfloat16 or wider, within the bound.
No kernel may reach another device: no remote copies, remote signals or barrier semaphores. Data moves between devices by JAX's collectives and lax.ppermute only.
A program may use at most 64 MiB of HBM per device.

```python
import math
import jax
import jax.numpy as jnp
import numpy as np
from jax import lax

HEADS = 20
HD = 128
BINS = 8
LOADERS = 128
GROUP_TOK = 512
TOKENS = 16384
BLK = 1
NBLK = 16384
N_DP = 32


def shared_rows(key):
    base = jnp.clip(jax.random.normal(jax.random.fold_in(key, 5), (TOKENS, HEADS * HD), jnp.float32), -5.0, 5.0)
    picked = jax.random.randint(jax.random.fold_in(key, 6), (TOKENS,), 0, 8) == 0
    strength = 10.0 * jax.random.randint(jax.random.fold_in(key, 7), (TOKENS, 1), 1, 4).astype(jnp.float32)
    return (base, picked, strength)


def draw_key_rows(key, part):
    base, picked, strength = shared_rows(key)
    key = jax.random.fold_in(key, 21)
    row_ids = jnp.arange(TOKENS, dtype=jnp.int32)
    offset = row_ids % BLK
    first_row = row_ids - offset
    spread = jax.random.uniform(key, (TOKENS, 1), jnp.float32, 1.5, 2.5)
    ripple = spread / (strength[first_row] * math.sqrt(HD))
    paired = (offset == 1) & picked[first_row]
    moved = jnp.clip(base[first_row] * (1.0 + ripple), -5.0, 5.0)
    values = jnp.where(paired[:, None], moved, base)
    return values.astype(jnp.bfloat16)


def draw_queries(key, part):
    base, picked, strength = shared_rows(key)
    key = jax.random.fold_in(key, 22)
    row_ids = jnp.arange(TOKENS, dtype=jnp.int32)
    offset = row_ids % BLK
    fresh = jnp.clip(jax.random.normal(key, (TOKENS, HEADS * HD), jnp.float32), -5.0, 5.0)
    aligned = (offset == 0) & picked
    strong = jnp.clip(strength * base, -80.0, 80.0)
    values = jnp.where(aligned[:, None], strong, fresh)
    return values.astype(jnp.bfloat16)


def draw_block_source(key, part):
    key = jax.random.fold_in(key, 23)
    owner_keys = jax.random.split(jax.random.fold_in(key, 1), LOADERS)
    loader_keys = jax.random.split(jax.random.fold_in(key, 2), LOADERS)
    sigma = jax.vmap(lambda sub_key: jax.random.permutation(sub_key, LOADERS))(owner_keys)
    tau = jax.vmap(lambda sub_key: jax.random.permutation(sub_key, LOADERS))(loader_keys)
    owner_ids = jnp.arange(LOADERS, dtype=jnp.int32)[:, None]
    loader_slot = tau[sigma, owner_ids]
    return (sigma * LOADERS + loader_slot).astype(jnp.int32).reshape(NBLK)


def with_ends(values, stream_key, low, top_value):
    dims = values.shape
    index_at = [jax.random.randint(jax.random.fold_in(stream_key, axis), (), 0, dims[axis]) for axis in range(len(dims))]
    values = values.at[tuple(index_at)].set(low)
    longest = dims.index(max(dims))
    index_at[longest] = (index_at[longest] + 1) % dims[longest]
    return values.at[tuple(index_at)].set(top_value)


def level_of(stream_key, shape, pieces, smallest, high):
    gain, own = 1.0, jax.random.fold_in(stream_key, 6)
    for axis_at, blocks in pieces:
        steps = jnp.exp(jax.random.uniform(jax.random.fold_in(own, axis_at), (blocks,), jnp.float32, smallest / len(pieces), high / len(pieces)))
        gain = gain * jnp.repeat(steps, shape[axis_at] // blocks).reshape([-1 if axis == axis_at else 1 for axis in range(len(shape))])
    return gain


def length_profile(count, total, limit, slope):
    weights = [(1 << 20) // math.isqrt(rank ** slope) + 1 for rank in range(2, count + 1)]
    spare, given = total - limit - (count - 1), [1] * (count - 1)
    while spare > 0:
        free = [i for i in range(count - 1) if given[i] < limit]
        whole, budget = sum([weights[i] for i in free]), spare
        for i in free:
            addition = min(limit - given[i], max(1, budget * weights[i] // whole), spare)
            given[i] = given[i] + addition
            spare = spare - addition
    return np.array([limit] + given)


def ragged(rng, amount, total, reach, lean):
    if amount == 2:
        one = jax.random.randint(rng, (), max(1, total - reach), min(reach, total - 1) + 1)
        return jnp.stack([one, total - one])
    tallies = jnp.asarray(length_profile(amount, total, reach, lean), jnp.int32)
    couples = (amount - 1) // 2
    donor, receiver = tallies[1:1 + 2 * couples:2], tallies[2:2 + 2 * couples:2]
    slack = jnp.minimum(donor - 1, reach - receiver)
    moved = jax.random.randint(jax.random.fold_in(rng, 1), (couples,), 0, 1 << 20) % (slack + 1)
    tallies = tallies.at[1:1 + 2 * couples:2].set(donor - moved).at[2:2 + 2 * couples:2].set(receiver + moved)
    return tallies[jax.random.permutation(jax.random.fold_in(rng, 2), amount)]


def normal_values(own_key, extent, deviation, limit, cuts=(), held_as=jnp.bfloat16):
    gain = level_of(own_key, extent, cuts, -0.22, 0.18) if cuts else 1.0
    entries = jax.random.normal(own_key, extent, jnp.float32) * deviation * gain
    return jnp.minimum(jnp.maximum(entries, -limit), limit).astype(held_as)


def setup_inputs(seed: int = 0) -> dict:
    keys = jax.random.split(jax.random.key(seed), 10)
    queries = draw_queries(jax.random.fold_in(keys[9], 71), 0)
    key_rows = draw_key_rows(jax.random.fold_in(keys[9], 71), 0)
    value_rows = normal_values(keys[2], (TOKENS, HEADS * HD), 1.0, 6.0, ((0, 128),))
    cotangent = normal_values(keys[3], (TOKENS, HEADS * HD), 1.0, 6.0, ((0, 128),))
    lengths = ragged(keys[4], N_DP, N_DP * GROUP_TOK * 5 // 8, GROUP_TOK, 2).astype(jnp.int32)
    sample_plan = jax.random.permutation(keys[5], N_DP).astype(jnp.int32)
    guide_bins = with_ends(jax.random.randint(keys[6], (N_DP,), 0, BINS), jax.random.fold_in(keys[6], 1), 0, BINS - 1).astype(jnp.int32)
    guide_table = jnp.clip(jax.random.uniform(keys[7], (BINS, HEADS), jnp.float32, 0.5, 2.0), 0.5, 2.0)
    block_source = draw_block_source(jax.random.fold_in(keys[9], 71), 0)
    return {"queries": queries, "key_rows": key_rows, "value_rows": value_rows, "cotangent": cotangent, "lengths": lengths, "sample_plan": sample_plan, "guide_bins": guide_bins, "guide_table": guide_table, "block_source": block_source}


def head_pass(query_head, key_head, value_head, grad_head, query_live, key_live):
    scores = jnp.dot(query_head, key_head.T, preferred_element_type=jnp.float32) * (HD ** -0.5)
    masked = jnp.where(key_live[None, :], scores, -1e30)
    top_score = jnp.max(masked, axis=1, keepdims=True)
    shifted_exp = jnp.where(key_live[None, :], jnp.exp(masked - top_score), 0.0)
    row_total = jnp.sum(shifted_exp, axis=1, keepdims=True)
    attend = jnp.where(query_live[:, None], shifted_exp / row_total, 0.0)
    attend_bf = attend.astype(jnp.bfloat16)
    output = jnp.dot(attend_bf, value_head, preferred_element_type=jnp.float32)
    grad_attend = jnp.dot(grad_head, value_head.T, preferred_element_type=jnp.float32)
    row_dot = jnp.sum(grad_head.astype(jnp.float32) * output, axis=1, keepdims=True)
    grad_scores = (attend * (grad_attend - row_dot) * (HD ** -0.5)).astype(jnp.bfloat16)
    grad_query = jnp.dot(grad_scores, key_head, preferred_element_type=jnp.float32)
    grad_key = jnp.dot(grad_scores.T, query_head, preferred_element_type=jnp.float32)
    grad_value = jnp.dot(attend_bf.T, grad_head, preferred_element_type=jnp.float32)
    return output, grad_query, grad_key, grad_value


def reference(queries, key_rows, value_rows, cotangent, lengths, sample_plan, guide_bins, guide_table, block_source):
    row_width = HEADS * HD

    def owned(source):
        return source.reshape(NBLK, BLK, row_width)[block_source].reshape(N_DP, GROUP_TOK, HEADS, HD)

    group_len = jnp.zeros((N_DP,), jnp.int32).at[sample_plan].set(lengths)
    group_bin = jnp.zeros((N_DP,), jnp.int32).at[sample_plan].set(guide_bins)
    head_gates = guide_table[group_bin]
    grad_own = (head_gates[:, None, :, None] * cotangent.reshape(N_DP, GROUP_TOK, HEADS, HD).astype(jnp.float32)).astype(jnp.bfloat16)

    def group_pass(group_items):
        query_group, key_group, value_group, grad_group, length_group = group_items
        live_rows = jnp.arange(GROUP_TOK, dtype=jnp.int32) < length_group

        def one_head(head_items):
            results = head_pass(head_items[0], head_items[1], head_items[2], head_items[3], live_rows, live_rows)
            return tuple(result.astype(jnp.bfloat16) for result in results)

        stacked = tuple(jnp.moveaxis(source, 1, 0) for source in (query_group, key_group, value_group, grad_group))
        results = lax.map(one_head, stacked)
        return tuple(jnp.moveaxis(result, 0, 1) for result in results)

    out_bf, grad_q, grad_k, grad_v = lax.map(group_pass, (owned(queries), owned(key_rows), owned(value_rows), grad_own, group_len))
    attn_out = (head_gates[:, None, :, None] * lax.optimization_barrier(out_bf).astype(jnp.float32)).astype(jnp.bfloat16).reshape(TOKENS, row_width)

    def loader_layout(source):
        blocks = source.reshape(NBLK, BLK, row_width)
        return jnp.zeros((NBLK, BLK, row_width), jnp.bfloat16).at[block_source].set(blocks).reshape(TOKENS, row_width)

    return attn_out, loader_layout(grad_q), loader_layout(grad_k), loader_layout(grad_v)
```

```python
import functools

import jax
import jax.numpy as jnp
from jax import lax
from jax.experimental import pallas as pl
from jax.experimental.pallas import tpu as pltpu
from jax.sharding import PartitionSpec as P

HEADS = 20
HD = 128
N_DP = 32
N_SP = 4
LOADERS = N_DP * N_SP
ROWS = 128
GROUP = 512
HEADS_DEV = HEADS // N_SP
WIDTH = HEADS * HD
PART = HEADS_DEV * HD
SCALE = HD ** (-0.5)
LOG2E = 1.4426950408889634
BF = jnp.bfloat16
F32 = jnp.float32
UNITS = 4
CHUNK = 16 * UNITS
VMEM_LIMIT = 48 * 1024 * 1024


def dot(a, b):
    return jnp.dot(a, b, preferred_element_type=F32)


def dot_nt(a, b):
    return lax.dot_general(a, b, (((1,), (1,)), ((), ())), preferred_element_type=F32)


def dot_tn(a, b):
    return lax.dot_general(a, b, (((0,), (0,)), ((), ())), preferred_element_type=F32)


def swap16():
    row = lax.broadcasted_iota(jnp.int32, (256, 256), 0)
    col = lax.broadcasted_iota(jnp.int32, (256, 256), 1)
    return jnp.where(col == (row % 16) * 16 + row // 16, 1.0, 0.0).astype(BF)


def combos(unit):
    for place in range(4):
        index = unit * 4 + place
        if index < 3 * HEADS_DEV:
            yield place, index // HEADS_DEV, index % HEADS_DEV


def row_picker(table_ref, me):
    table = table_ref[...]
    slot = jnp.sum(jnp.where(table // ROWS == me, table % ROWS, 0), axis=1, keepdims=True)
    lane = lax.broadcasted_iota(jnp.int32, (LOADERS, ROWS), 1)
    row = lax.broadcasted_iota(jnp.int32, (LOADERS, ROWS), 0)
    pick = jnp.where(slot == lane, 1.0, 0.0).astype(BF)
    order = jnp.where(lane == (row % N_DP) * N_SP + row // N_DP, 1.0, 0.0).astype(BF)
    return dot(order, pick).astype(BF)


def source_onehot(table_row):
    loader = lax.broadcasted_iota(jnp.int32, (LOADERS, ROWS), 0)
    return jnp.where(table_row // ROWS == loader, 1.0, 0.0).astype(BF)


def pack_kernel(me_ref, table_ref, q_ref, k_ref, v_ref, send_ref, rows_ref):
    pick = row_picker(table_ref, me_ref[0])
    for array, ref in enumerate((q_ref, k_ref, v_ref)):
        rows_ref[array] = dot(pick, ref[...]).astype(BF)
    swap = swap16()
    for part in range(N_SP):
        for half in range(2):
            blocks = []
            for unit in range(UNITS):
                pieces = []
                for _, array, head in combos(unit):
                    lanes = pl.ds((part * HEADS_DEV + head) * HD, HD)
                    for quarter in range(4):
                        pieces.append(rows_ref[array, pl.ds(quarter * N_DP + half * 16, 16), lanes])
                if len(pieces) < 16:
                    pieces.append(jnp.zeros((256 - 16 * len(pieces), HD), BF))
                blocks.append(jnp.concatenate(pieces, axis=0))
            for pair in range(UNITS // 2):
                both = jnp.concatenate(blocks[2 * pair : 2 * pair + 2], axis=1)
                swapped = dot(swap, both).astype(BF)
                for side in range(2):
                    unit = 2 * pair + side
                    for group in range(16):
                        send_ref[(half * 16 + group) * N_SP + part, pl.ds(unit * 16, 16), :] = swapped[
                            group * 16 : (group + 1) * 16, side * HD : (side + 1) * HD
                        ]


def unpack_kernel(me_ref, table_ref, recv_ref, q_ref, k_ref, v_ref, rows_ref):
    pick = row_picker(table_ref, me_ref[0])
    swap = swap16()
    for part in range(N_SP):
        for half in range(2):
            for pair in range(UNITS // 2):
                blocks = []
                for side in range(2):
                    unit = 2 * pair + side
                    blocks.append(
                        jnp.concatenate(
                            [
                                recv_ref[(half * 16 + group) * N_SP + part, pl.ds(unit * 16, 16), :]
                                for group in range(16)
                            ],
                            axis=0,
                        )
                    )
                swapped = dot(swap, jnp.concatenate(blocks, axis=1)).astype(BF)
                for side in range(2):
                    for place, array, head in combos(2 * pair + side):
                        lanes = pl.ds((part * HEADS_DEV + head) * HD, HD)
                        for quarter in range(4):
                            at = (place * 4 + quarter) * 16
                            rows_ref[array, pl.ds(quarter * N_DP + half * 16, 16), lanes] = swapped[
                                at : at + 16, side * HD : (side + 1) * HD
                            ]
    for array, ref in enumerate((q_ref, k_ref, v_ref)):
        ref[...] = dot_tn(pick, rows_ref[array]).astype(BF)


def part_lanes(index):
    return pl.ds(pl.multiple_of(index * PART, HD), PART)


def spread_kernel(me_ref, table_ref, cot_ref, *out_refs):
    me = me_ref[0]
    onehot = source_onehot(table_ref[pl.ds(me, 1), :])
    for step in range(N_SP):
        other = jnp.bitwise_xor(me % N_SP, step)
        out_refs[step][...] = dot(onehot, cot_ref[:, part_lanes(other)]).astype(BF)


def collect_kernel(me_ref, table_ref, *refs):
    in_refs, out_ref = refs[:-1], refs[-1]
    me = me_ref[0]
    onehot = source_onehot(table_ref[pl.ds(me, 1), :])
    for step in range(N_SP):
        other = jnp.bitwise_xor(me % N_SP, step)
        out_ref[:, part_lanes(other)] = dot_tn(onehot, in_refs[step][...]).astype(BF)


def attend_kernel(
    me_ref,
    lengths_ref,
    plan_ref,
    bins_ref,
    guide_ref,
    table_ref,
    recv_ref,
    d0_ref,
    d1_ref,
    d2_ref,
    d3_ref,
    ret_ref,
    o0_ref,
    o1_ref,
    o2_ref,
    o3_ref,
    items_ref,
    cot_ref,
    out_ref,
    bias_ref,
    live_ref,
):
    me = me_ref[0]
    group = me // N_SP
    mine = me % N_SP
    group_len = jnp.int32(0)
    group_bin = jnp.int32(0)
    for sample in range(N_DP):
        hit = plan_ref[sample] == group
        group_len = jnp.where(hit, lengths_ref[sample], group_len)
        group_bin = jnp.where(hit, bins_ref[sample], group_bin)
    for quarter in range(4):
        onehot = source_onehot(table_ref[pl.ds(group * N_SP + quarter, 1), :])
        lane = lax.broadcasted_iota(jnp.int32, (LOADERS, ROWS), 1).astype(F32)
        limit = (group_len - quarter * ROWS).astype(F32)
        where_col = jnp.sum(onehot.astype(F32) * lane, axis=1, keepdims=True)
        where_row = dot_nt(lane[:8].astype(BF), onehot)
        bias_ref[pl.ds(quarter * ROWS, ROWS), :] = jnp.broadcast_to(
            jnp.where(where_col < limit, 0.0, -1e30), (ROWS, HD)
        )
        live_ref[:, pl.ds(quarter * ROWS, ROWS)] = jnp.where(where_row < limit, 1.0, 0.0)
    for step, ref in enumerate((d0_ref, d1_ref, d2_ref, d3_ref)):
        source = jnp.bitwise_xor(mine, step)
        cot_ref[pl.ds(pl.multiple_of(source * ROWS, ROWS), ROWS), :] = ref[...]
    swap = swap16()
    for block in range(8):
        for pair in range(UNITS // 2):
            both = jnp.concatenate(
                [
                    recv_ref[pl.ds(block * 16, 16), pl.ds((2 * pair + side) * 16, 16), :].reshape(256, HD)
                    for side in range(2)
                ],
                axis=1,
            )
            swapped = dot(swap, both).astype(BF)
            for side in range(2):
                unit = 2 * pair + side
                for place in range(4):
                    for quarter in range(4):
                        at = (place * 4 + quarter) * 16
                        items_ref[unit * 4 + place, pl.ds(quarter * ROWS + block * 16, 16), :] = swapped[
                            at : at + 16, side * HD : (side + 1) * HD
                        ]
    live = live_ref[0:1, :]
    bias = bias_ref[:, 0:1]
    for head in range(HEADS_DEV):
        gate = guide_ref[group_bin, mine * HEADS_DEV + head]
        query = items_ref[head]
        key = items_ref[HEADS_DEV + head]
        value = items_ref[2 * HEADS_DEV + head]
        lanes = pl.ds(head * HD, HD)
        grad = (gate * cot_ref[:, lanes].astype(F32)).astype(BF)
        scores = dot_nt(key, query) + bias
        top = jnp.max(scores, axis=0, keepdims=True)
        raised = jnp.exp2((scores - top) * (SCALE * LOG2E))
        attend = raised * (live / jnp.sum(raised, axis=0, keepdims=True))
        attend_bf = attend.astype(BF)
        output = dot_tn(attend_bf, value)
        grad_attend = dot_nt(value, grad)
        row_dot = jnp.sum((grad.astype(F32) * output).T, axis=0, keepdims=True)
        grad_scores = (attend * (grad_attend - row_dot) * SCALE).astype(BF)
        out_ref[:, lanes] = (gate * output.astype(BF).astype(F32)).astype(BF)
        items_ref[2 * HEADS_DEV + head] = dot(attend_bf, grad).astype(BF)
        items_ref[head] = dot_tn(grad_scores, key).astype(BF)
        items_ref[HEADS_DEV + head] = dot(grad_scores, query).astype(BF)
    for step, ref in enumerate((o0_ref, o1_ref, o2_ref, o3_ref)):
        target = jnp.bitwise_xor(mine, step)
        ref[...] = out_ref[pl.ds(pl.multiple_of(target * ROWS, ROWS), ROWS), :]
    for block in range(8):
        for pair in range(UNITS // 2):
            both = jnp.concatenate(
                [
                    jnp.concatenate(
                        [
                            items_ref[
                                (2 * pair + side) * 4 + place, pl.ds(quarter * ROWS + block * 16, 16), :
                            ]
                            for place in range(4)
                            for quarter in range(4)
                        ],
                        axis=0,
                    )
                    for side in range(2)
                ],
                axis=1,
            )
            swapped = dot(swap, both).astype(BF)
            for side in range(2):
                ret_ref[pl.ds(block * 16, 16), pl.ds((2 * pair + side) * 16, 16), :] = swapped[
                    :, side * HD : (side + 1) * HD
                ].reshape(16, 16, HD)


SMEM = pl.BlockSpec(memory_space=pltpu.SMEM)
VMEM = pl.BlockSpec(memory_space=pltpu.VMEM)
PARAMS = pltpu.CompilerParams(vmem_limit_bytes=VMEM_LIMIT)
CHUNKS = jax.ShapeDtypeStruct((LOADERS, CHUNK, HD), BF)
PIECE = jax.ShapeDtypeStruct((ROWS, PART), BF)
WHOLE = jax.ShapeDtypeStruct((ROWS, WIDTH), BF)


def pack(me, table, queries, keys, values):
    return pl.pallas_call(
        pack_kernel,
        out_shape=CHUNKS,
        in_specs=[SMEM] + [VMEM] * 4,
        out_specs=VMEM,
        scratch_shapes=[pltpu.VMEM((3, ROWS, WIDTH), BF)],
        compiler_params=PARAMS,
        name="pack",
    )(me, table, queries, keys, values)


def unpack(me, table, chunks):
    return pl.pallas_call(
        unpack_kernel,
        out_shape=(WHOLE,) * 3,
        in_specs=[SMEM] + [VMEM] * 2,
        out_specs=(VMEM,) * 3,
        scratch_shapes=[pltpu.VMEM((3, ROWS, WIDTH), BF)],
        compiler_params=PARAMS,
        name="unpack",
    )(me, table, chunks)


def spread(me, table, cotangent):
    return pl.pallas_call(
        spread_kernel,
        out_shape=(PIECE,) * N_SP,
        in_specs=[SMEM] + [VMEM] * 2,
        out_specs=(VMEM,) * N_SP,
        compiler_params=PARAMS,
        name="spread",
    )(me, table, cotangent)


def collect(me, table, pieces):
    return pl.pallas_call(
        collect_kernel,
        out_shape=WHOLE,
        in_specs=[SMEM] + [VMEM] * (1 + N_SP),
        out_specs=VMEM,
        compiler_params=PARAMS,
        name="collect",
    )(me, table, *pieces)


def attend(me, lengths, plan, bins, guide, table, chunks, pieces):
    return pl.pallas_call(
        attend_kernel,
        out_shape=(CHUNKS,) + (PIECE,) * N_SP,
        in_specs=[SMEM] * 5 + [VMEM] * (2 + N_SP),
        out_specs=(VMEM,) * (1 + N_SP),
        scratch_shapes=[
            pltpu.VMEM((16, GROUP, HD), BF),
            pltpu.VMEM((GROUP, PART), BF),
            pltpu.VMEM((GROUP, PART), BF),
            pltpu.VMEM((GROUP, HD), F32),
            pltpu.VMEM((8, GROUP), F32),
        ],
        compiler_params=PARAMS,
        name="attend",
    )(me, lengths, plan, bins, guide, table, chunks, *pieces)


def exchange(chunks):
    return lax.all_to_all(chunks, ("dp", "sp"), split_axis=0, concat_axis=0, tiled=True)


def swap_pieces(pieces):
    moved = [pieces[0]]
    for step in range(1, N_SP):
        moved.append(lax.ppermute(pieces[step], "sp", [(i, i ^ step) for i in range(N_SP)]))
    return moved


def per_device(
    queries,
    key_rows,
    value_rows,
    cotangent,
    lengths,
    sample_plan,
    guide_bins,
    guide_table,
    block_source,
):
    me = (lax.axis_index("dp") * N_SP + lax.axis_index("sp")).astype(jnp.int32).reshape(1)
    table = block_source.reshape(LOADERS, ROWS)
    grad_pieces = swap_pieces(spread(me, table, cotangent))
    chunks = exchange(pack(me, table, queries, key_rows, value_rows))
    results = attend(
        me, lengths, sample_plan, guide_bins, guide_table, table, chunks, grad_pieces
    )
    out_pieces = swap_pieces(results[1:])
    back = exchange(results[0])
    grad_queries, grad_keys, grad_values = unpack(me, table, back)
    attn_out = collect(me, table, out_pieces)
    return attn_out, grad_queries, grad_keys, grad_values


def solution(mesh):
    rows = P(("dp", "sp"), None)
    return jax.shard_map(
        per_device,
        mesh=mesh,
        in_specs=(rows,) * 4 + (P(),) * 5,
        out_specs=(rows,) * 4,
        check_vma=False,
    )
```

```python
import jax
import jax.numpy as jnp
from jax import lax
from jax.experimental import pallas as pl
from jax.experimental.pallas import tpu as pltpu
from jax.sharding import PartitionSpec as P

HEADS = 20
HD = 128
N_DP = 32
N_SP = 4
LOADERS = N_DP * N_SP
ROWS = 128
GROUP = 512
HEADS_DEV = HEADS // N_SP
WIDTH = HEADS * HD
PART = HEADS_DEV * HD
CHUNK = 3 * PART
SCALE = HD ** (-0.5)
LOG2E = 1.4426950408889634
BF = jnp.bfloat16
F32 = jnp.float32


def dot(a, b):
    return jnp.dot(a, b, preferred_element_type=F32)


def dot_nt(a, b):
    return lax.dot_general(a, b, (((1,), (1,)), ((), ())), preferred_element_type=F32)


def dot_tn(a, b):
    return lax.dot_general(a, b, (((0,), (0,)), ((), ())), preferred_element_type=F32)


def iota(shape, dim):
    return lax.broadcasted_iota(jnp.int32, shape, dim)


def onehot(hit):
    return jnp.where(hit, 1.0, 0.0).astype(BF)


def row_picker(table, me):
    slot = jnp.sum(jnp.where(table // ROWS == me, table % ROWS, 0), axis=1, keepdims=True)
    return onehot(slot == iota((LOADERS, ROWS), 1))


def quarters_first():
    row, col = iota((256, 256), 0), iota((256, 256), 1)
    return onehot(col == (row % 64) * 4 + row // 64)


def columns(head, array):
    return pl.ds((head * 3 + array) * HD, HD)


def part_lanes(index):
    return pl.ds(pl.multiple_of(index * PART, HD), PART)


def sample_of(group, plan_ref, value_ref):
    value = jnp.int32(0)
    for sample in range(N_DP):
        value = jnp.where(plan_ref[sample] == group, value_ref[sample], value)
    return value


def pack_kernel(me_ref, table_ref, q_ref, k_ref, v_ref, out_ref, index_ref, in_ref, send_ref, table_sem, in_sem, out_sem):
    index = pltpu.make_async_copy(table_ref, index_ref, table_sem)
    index.start()
    loads = []
    for part in range(N_SP):
        lanes = pl.ds(part * PART, PART)
        for array, ref in enumerate((q_ref, k_ref, v_ref)):
            load = pltpu.make_async_copy(ref.at[:, lanes], in_ref.at[array, :, lanes], in_sem.at[part, array])
            load.start()
            loads.append(load)
    index.wait()
    pick = row_picker(index_ref[...], me_ref[0])
    stores = []
    for part in range(N_SP):
        for array in range(3):
            loads[part * 3 + array].wait()
            rows = dot(pick, in_ref[array, :, pl.ds(part * PART, PART)]).astype(BF).reshape(N_DP, 4, PART)
            for head in range(HEADS_DEV):
                send_ref[part, :, :, columns(head, array)] = rows[:, :, head * HD : (head + 1) * HD]
        store = pltpu.make_async_copy(send_ref.at[part], out_ref.at[:, part], out_sem.at[part])
        store.start()
        stores.append(store)
    for store in stores:
        store.wait()


def unpack_kernel(pick_ref, recv_ref, q_ref, k_ref, v_ref, out_ref, out_sem):
    pick = pick_ref[...]
    stores = []
    for part in range(N_SP):
        lanes = pl.ds(part * PART, PART)
        for array, ref in enumerate((q_ref, k_ref, v_ref)):
            rows = jnp.concatenate(
                [recv_ref[:, part, :, columns(head, array)].reshape(ROWS, HD) for head in range(HEADS_DEV)],
                axis=1,
            )
            out_ref[array, :, lanes] = dot(pick, rows).astype(BF)
            store = pltpu.make_async_copy(
                out_ref.at[array, :, lanes], ref.at[:, lanes], out_sem.at[array, part]
            )
            store.start()
            stores.append(store)
    for store in stores:
        store.wait()


def spread_kernel(
    me_ref,
    lengths_ref,
    plan_ref,
    bins_ref,
    guide_ref,
    table_ref,
    cot_ref,
    p0_ref,
    p1_ref,
    p2_ref,
    p3_ref,
    bias_ref,
    live_ref,
    pick_ref,
    gated_ref,
):
    me = me_ref[0]
    group, mine = me // N_SP, me % N_SP
    group_len = sample_of(group, plan_ref, lengths_ref)
    group_bin = sample_of(group, plan_ref, bins_ref)
    for head in range(HEADS):
        lanes = pl.ds(head * HD, HD)
        gated_ref[:, lanes] = (guide_ref[group_bin, head] * cot_ref[:, lanes].astype(F32)).astype(BF)
    order = onehot(table_ref[pl.ds(me, 1), :] // ROWS == iota((LOADERS, ROWS), 0))
    for step, ref in enumerate((p0_ref, p1_ref, p2_ref, p3_ref)):
        ref[...] = dot(order, gated_ref[:, part_lanes(jnp.bitwise_xor(mine, step))]).astype(BF)
    pick_ref[...] = row_picker(table_ref[...], me).astype(F32).T.astype(BF)
    row = iota((GROUP, ROWS), 0)
    source = jnp.zeros((GROUP, ROWS), jnp.int32)
    for quarter in range(4):
        own = table_ref[pl.ds(group * N_SP + quarter, 1), :] // ROWS
        source = jnp.where(row % 4 == quarter, own, source)
    place = onehot(source == row // 4)
    count = iota((ROWS, HD), 0).astype(F32).astype(BF)
    place_col = dot(place, count) + (ROWS * (row % 4)).astype(F32)
    bias_ref[...] = jnp.where(place_col < group_len.astype(F32), 0.0, -1e30)
    lane = iota((8, GROUP), 1)
    place_row = dot_nt(iota((8, ROWS), 1).astype(F32).astype(BF), place) + (ROWS * (lane % 4)).astype(F32)
    live_ref[...] = jnp.where(place_row < group_len.astype(F32), 1.0, 0.0)


def collect_kernel(me_ref, plan_ref, bins_ref, guide_ref, table_ref, i0_ref, i1_ref, i2_ref, i3_ref, out_ref):
    me = me_ref[0]
    group, mine = me // N_SP, me % N_SP
    group_bin = sample_of(group, plan_ref, bins_ref)
    order = onehot(table_ref[pl.ds(me, 1), :] // ROWS == iota((LOADERS, ROWS), 0)).astype(F32).T.astype(BF)
    for step, ref in enumerate((i0_ref, i1_ref, i2_ref, i3_ref)):
        out_ref[:, part_lanes(jnp.bitwise_xor(mine, step))] = dot(order, ref[...]).astype(BF)
    for head in range(HEADS):
        lanes = pl.ds(head * HD, HD)
        out_ref[:, lanes] = (guide_ref[group_bin, head] * out_ref[:, lanes].astype(F32)).astype(BF)


def forward_kernel(
    me_ref, bias_ref, live_ref, recv_ref, raised_ref, inverse_ref, o0_ref, o1_ref, o2_ref, o3_ref, out_ref
):
    mine = me_ref[0] % N_SP
    live = live_ref[0:1, :]
    bias = bias_ref[:, 0:1]
    order = quarters_first()
    for head in range(HEADS_DEV):
        query = recv_ref[:, :, columns(head, 0)].reshape(GROUP, HD)
        key = recv_ref[:, :, columns(head, 1)].reshape(GROUP, HD)
        value = recv_ref[:, :, columns(head, 2)].reshape(GROUP, HD)
        scores = dot_nt(key, query) + bias
        top = jnp.max(scores, axis=0, keepdims=True)
        raised = jnp.exp2((scores - top) * (SCALE * LOG2E))
        inverse = live / jnp.sum(raised, axis=0, keepdims=True)
        weights = raised.astype(BF)
        raised_ref[head] = weights
        inverse_ref[head : head + 1, :] = inverse
        output = (dot_tn(value, weights) * inverse).astype(BF)
        for half in range(2):
            rows = dot_nt(order, output[:, half * 256 : (half + 1) * 256]).astype(BF)
            out_ref[:, pl.ds(half * 64, 64), pl.ds(head * HD, HD)] = rows.reshape(4, 64, HD)
    inverse_ref[HEADS_DEV:, :] = jnp.zeros((8 - HEADS_DEV, GROUP), F32)
    for step, ref in enumerate((o0_ref, o1_ref, o2_ref, o3_ref)):
        ref[...] = out_ref[jnp.bitwise_xor(mine, step)]


def backward_kernel(
    me_ref, recv_ref, raised_ref, inverse_ref, d0_ref, d1_ref, d2_ref, d3_ref, ret_ref, cot_ref, grad_ref
):
    mine = me_ref[0] % N_SP
    for step, ref in enumerate((d0_ref, d1_ref, d2_ref, d3_ref)):
        cot_ref[jnp.bitwise_xor(mine, step)] = ref[...]
    order = quarters_first()
    for half in range(2):
        rows = cot_ref[:, pl.ds(half * 64, 64), :].reshape(256, PART)
        grad_ref[pl.ds(half * 256, 256), :] = dot_tn(order, rows).astype(BF)
    inverse_columns = inverse_ref[...].T
    for head in range(HEADS_DEV):
        query = recv_ref[:, :, columns(head, 0)].reshape(GROUP, HD)
        key = recv_ref[:, :, columns(head, 1)].reshape(GROUP, HD)
        value = recv_ref[:, :, columns(head, 2)].reshape(GROUP, HD)
        inverse = inverse_ref[head : head + 1, :]
        scale = inverse_columns[:, head : head + 1] * SCALE
        grad = (grad_ref[:, pl.ds(head * HD, HD)].astype(F32) * scale).astype(BF)
        weights = raised_ref[head]
        wide = weights.astype(F32)
        grad_attend = dot_nt(value, grad)
        row_dot = jnp.sum(wide * grad_attend, axis=0, keepdims=True) * inverse
        grad_scores = (wide * (grad_attend - row_dot)).astype(BF)
        grad_query = dot_tn(key, grad_scores).T.astype(BF)
        grad_key = dot(grad_scores, query).astype(BF)
        grad_value = (dot(weights, grad) * (1.0 / SCALE)).astype(BF)
        ret_ref[:, :, columns(head, 0)] = grad_query.reshape(LOADERS, 4, HD)
        ret_ref[:, :, columns(head, 1)] = grad_key.reshape(LOADERS, 4, HD)
        ret_ref[:, :, columns(head, 2)] = grad_value.reshape(LOADERS, 4, HD)


SMEM = pl.BlockSpec(memory_space=pltpu.SMEM)
VMEM = pl.BlockSpec(memory_space=pltpu.VMEM)
HBM = pl.BlockSpec(memory_space=pltpu.HBM)
PARAMS = pltpu.CompilerParams(vmem_limit_bytes=24 * 1024 * 1024)
PIECE = jax.ShapeDtypeStruct((ROWS, PART), BF)
WHOLE = jax.ShapeDtypeStruct((ROWS, WIDTH), BF)


def in_hbm(array):
    return pltpu.with_memory_space_constraint(array, pltpu.HBM)


def pack(me, table, queries, keys, values):
    chunks = pl.pallas_call(
        pack_kernel,
        out_shape=pltpu.HBM((N_DP, N_SP, 4, CHUNK), BF),
        in_specs=[SMEM] + [HBM] * 4,
        out_specs=HBM,
        scratch_shapes=[
            pltpu.VMEM((LOADERS, ROWS), jnp.int32),
            pltpu.VMEM((3, ROWS, WIDTH), BF),
            pltpu.VMEM((N_SP, N_DP, 4, CHUNK), BF),
            pltpu.SemaphoreType.DMA,
            pltpu.SemaphoreType.DMA((N_SP, 3)),
            pltpu.SemaphoreType.DMA((N_SP,)),
        ],
        compiler_params=PARAMS,
        name="pack",
    )(me, in_hbm(table), in_hbm(queries), in_hbm(keys), in_hbm(values))
    return chunks.reshape(LOADERS, 4, CHUNK)


def unpack(pick, chunks):
    return pl.pallas_call(
        unpack_kernel,
        out_shape=(pltpu.HBM((ROWS, WIDTH), BF),) * 3,
        in_specs=[VMEM] * 2,
        out_specs=(HBM,) * 3,
        scratch_shapes=[
            pltpu.VMEM((3, ROWS, WIDTH), BF),
            pltpu.SemaphoreType.DMA((3, N_SP)),
        ],
        compiler_params=PARAMS,
        name="unpack",
    )(pick, chunks.reshape(N_DP, N_SP, 4, CHUNK))


def spread(me, lengths, plan, bins, guide, table, cotangent):
    return pl.pallas_call(
        spread_kernel,
        out_shape=(PIECE,) * N_SP
        + (
            jax.ShapeDtypeStruct((GROUP, HD), F32),
            jax.ShapeDtypeStruct((8, GROUP), F32),
            jax.ShapeDtypeStruct((ROWS, LOADERS), BF),
        ),
        in_specs=[SMEM] * 5 + [VMEM] * 2,
        out_specs=(VMEM,) * (N_SP + 3),
        scratch_shapes=[pltpu.VMEM((ROWS, WIDTH), BF)],
        compiler_params=PARAMS,
        name="spread",
    )(me, lengths, plan, bins, guide, table, cotangent)


def collect(me, plan, bins, guide, table, pieces):
    return pl.pallas_call(
        collect_kernel,
        out_shape=WHOLE,
        in_specs=[SMEM] * 4 + [VMEM] * (1 + N_SP),
        out_specs=VMEM,
        compiler_params=PARAMS,
        name="collect",
    )(me, plan, bins, guide, table, *pieces)


def forward(me, bias, live, chunks):
    return pl.pallas_call(
        forward_kernel,
        out_shape=(
            jax.ShapeDtypeStruct((HEADS_DEV, GROUP, GROUP), BF),
            jax.ShapeDtypeStruct((8, GROUP), F32),
        )
        + (PIECE,) * N_SP,
        in_specs=[SMEM] + [VMEM] * 3,
        out_specs=(VMEM,) * (2 + N_SP),
        scratch_shapes=[pltpu.VMEM((4, ROWS, PART), BF)],
        compiler_params=PARAMS,
        name="forward",
    )(me, bias, live, chunks)


def backward(me, chunks, raised, inverse, pieces):
    return pl.pallas_call(
        backward_kernel,
        out_shape=jax.ShapeDtypeStruct((LOADERS, 4, CHUNK), BF),
        in_specs=[SMEM] + [VMEM] * (3 + N_SP),
        out_specs=VMEM,
        scratch_shapes=[
            pltpu.VMEM((4, ROWS, PART), BF),
            pltpu.VMEM((GROUP, PART), BF),
        ],
        compiler_params=PARAMS,
        name="backward",
    )(me, chunks, raised, inverse, *pieces)


def exchange(chunks):
    return lax.all_to_all(chunks, ("dp", "sp"), split_axis=0, concat_axis=0, tiled=True)


def swap_pieces(pieces):
    return [pieces[0]] + [
        lax.ppermute(pieces[step], "sp", [(i, i ^ step) for i in range(N_SP)]) for step in range(1, N_SP)
    ]


def per_device(
    queries,
    key_rows,
    value_rows,
    cotangent,
    lengths,
    sample_plan,
    guide_bins,
    guide_table,
    block_source,
):
    me = (lax.axis_index("dp") * N_SP + lax.axis_index("sp")).astype(jnp.int32).reshape(1)
    table = block_source.reshape(LOADERS, ROWS)
    chunks = exchange(pack(me, table, queries, key_rows, value_rows))
    *pieces, bias, live, pick = spread(
        me, lengths, sample_plan, guide_bins, guide_table, table, cotangent
    )
    chunks, pieces = lax.optimization_barrier((chunks, pieces))
    grad_pieces = swap_pieces(pieces)
    raised, inverse, *outs = forward(me, bias, live, chunks)
    out_pieces = swap_pieces(outs)
    grads = backward(me, chunks, raised, inverse, grad_pieces)
    grads, out_pieces[2], out_pieces[3] = lax.optimization_barrier((grads, out_pieces[2], out_pieces[3]))
    back = exchange(grads)
    attn_out = collect(me, sample_plan, guide_bins, guide_table, table, out_pieces)
    return attn_out, *unpack(pick, back)


def solution(mesh):
    rows = P(("dp", "sp"), None)
    return jax.shard_map(
        per_device,
        mesh=mesh,
        in_specs=(rows,) * 4 + (P(),) * 5,
        out_specs=(rows,) * 4,
        check_vma=False,
    )
```

```python
import jax
import jax.numpy as jnp
from jax import lax
from jax.experimental import pallas as pl
from jax.experimental.pallas import tpu as pltpu
from jax.sharding import PartitionSpec as P

HEADS = 20
HD = 128
N_DP = 32
N_SP = 4
LOADERS = N_DP * N_SP
ROWS = 128
GROUP = 512
HEADS_DEV = HEADS // N_SP
WIDTH = HEADS * HD
PART = HEADS_DEV * HD
CHUNK = 3 * PART
SCALE = HD ** (-0.5)
LOG2E = 1.4426950408889634
BF = jnp.bfloat16
F32 = jnp.float32


def dot(a, b):
    return jnp.dot(a, b, preferred_element_type=F32)


def dot_nt(a, b):
    return lax.dot_general(a, b, (((1,), (1,)), ((), ())), preferred_element_type=F32)


def dot_tn(a, b):
    return lax.dot_general(a, b, (((0,), (0,)), ((), ())), preferred_element_type=F32)


def iota(shape, dim):
    return lax.broadcasted_iota(jnp.int32, shape, dim)


def onehot(hit):
    return jnp.where(hit, 1.0, 0.0).astype(BF)


def row_picker(table, me):
    slot = jnp.sum(jnp.where(table // ROWS == me, table % ROWS, 0), axis=1, keepdims=True)
    return onehot(slot == iota((LOADERS, ROWS), 1))


def quarters_first():
    row, col = iota((256, 256), 0), iota((256, 256), 1)
    return onehot(col == (row % 64) * 4 + row // 64)


def columns(head, array):
    return pl.ds((array * HEADS_DEV + head) * HD, HD)


def part_lanes(index):
    return pl.ds(pl.multiple_of(index * PART, HD), PART)


def sample_of(group, plan_ref, value_ref):
    value = jnp.int32(0)
    for sample in range(N_DP):
        value = jnp.where(plan_ref[sample] == group, value_ref[sample], value)
    return value


def pack_kernel(me_ref, table_ref, q_ref, k_ref, v_ref, out_ref, index_ref, in_ref, send_ref, index_sem, in_sem, out_sem):
    index = pltpu.make_async_copy(table_ref, index_ref, index_sem)
    index.start()
    loads = []
    for array, ref in enumerate((q_ref, k_ref, v_ref)):
        load = pltpu.make_async_copy(ref, in_ref.at[array], in_sem.at[array])
        load.start()
        loads.append(load)
    index.wait()
    pick = row_picker(index_ref[...], me_ref[0])
    stores = []
    for array in range(3):
        loads[array].wait()
        lanes = pl.ds(array * PART, PART)
        for part in range(N_SP):
            rows = dot(pick, in_ref[array, :, pl.ds(part * PART, PART)]).astype(BF)
            send_ref[:, part, :, lanes] = rows.reshape(N_DP, 4, PART)
        store = pltpu.make_async_copy(
            send_ref.at[:, :, :, lanes], out_ref.at[:, :, :, lanes], out_sem.at[array]
        )
        store.start()
        stores.append(store)
    for store in stores:
        store.wait()


def unpack_kernel(pick_ref, recv_ref, q_ref, k_ref, v_ref, out_ref, out_sem):
    pick = pick_ref[...]
    stores = []
    for array, ref in enumerate((q_ref, k_ref, v_ref)):
        for part in range(N_SP):
            rows = recv_ref[:, part, :, pl.ds(array * PART, PART)].reshape(ROWS, PART)
            out_ref[array, :, pl.ds(part * PART, PART)] = dot(pick, rows).astype(BF)
        store = pltpu.make_async_copy(out_ref.at[array], ref, out_sem.at[array])
        store.start()
        stores.append(store)
    for store in stores:
        store.wait()


def spread_kernel(
    me_ref,
    lengths_ref,
    plan_ref,
    bins_ref,
    guide_ref,
    table_ref,
    cot_ref,
    p0_ref,
    p1_ref,
    p2_ref,
    p3_ref,
    bias_ref,
    live_ref,
    pick_ref,
    gated_ref,
):
    me = me_ref[0]
    group, mine = me // N_SP, me % N_SP
    group_len = sample_of(group, plan_ref, lengths_ref)
    group_bin = sample_of(group, plan_ref, bins_ref)
    for head in range(HEADS):
        lanes = pl.ds(head * HD, HD)
        gated_ref[:, lanes] = (guide_ref[group_bin, head] * cot_ref[:, lanes].astype(F32)).astype(BF)
    order = onehot(table_ref[pl.ds(me, 1), :] // ROWS == iota((LOADERS, ROWS), 0))
    for step, ref in enumerate((p0_ref, p1_ref, p2_ref, p3_ref)):
        ref[...] = dot(order, gated_ref[:, part_lanes(jnp.bitwise_xor(mine, step))]).astype(BF)
    pick_ref[...] = row_picker(table_ref[...], me).astype(F32).T.astype(BF)
    row = iota((GROUP, ROWS), 0)
    source = jnp.zeros((GROUP, ROWS), jnp.int32)
    for quarter in range(4):
        own = table_ref[pl.ds(group * N_SP + quarter, 1), :] // ROWS
        source = jnp.where(row % 4 == quarter, own, source)
    place = onehot(source == row // 4)
    count = iota((ROWS, HD), 0).astype(F32).astype(BF)
    place_col = dot(place, count) + (ROWS * (row % 4)).astype(F32)
    bias_ref[...] = jnp.where(place_col < group_len.astype(F32), 0.0, -1e30)
    lane = iota((8, GROUP), 1)
    place_row = dot_nt(iota((8, ROWS), 1).astype(F32).astype(BF), place) + (ROWS * (lane % 4)).astype(F32)
    live_ref[...] = jnp.where(place_row < group_len.astype(F32), 1.0, 0.0)


def collect_kernel(me_ref, plan_ref, bins_ref, guide_ref, table_ref, i0_ref, i1_ref, i2_ref, i3_ref, out_ref):
    me = me_ref[0]
    group, mine = me // N_SP, me % N_SP
    group_bin = sample_of(group, plan_ref, bins_ref)
    order = onehot(table_ref[pl.ds(me, 1), :] // ROWS == iota((LOADERS, ROWS), 0)).astype(F32).T.astype(BF)
    for step, ref in enumerate((i0_ref, i1_ref, i2_ref, i3_ref)):
        out_ref[:, part_lanes(jnp.bitwise_xor(mine, step))] = dot(order, ref[...]).astype(BF)
    for head in range(HEADS):
        lanes = pl.ds(head * HD, HD)
        out_ref[:, lanes] = (guide_ref[group_bin, head] * out_ref[:, lanes].astype(F32)).astype(BF)


def forward_kernel(
    me_ref, bias_ref, live_ref, recv_ref, raised_ref, inverse_ref, o0_ref, o1_ref, o2_ref, o3_ref, out_ref
):
    mine = me_ref[0] % N_SP
    live = live_ref[0:1, :]
    bias = bias_ref[:, 0:1]
    order = quarters_first()
    for head in range(HEADS_DEV):
        query = recv_ref[:, :, columns(head, 0)].reshape(GROUP, HD)
        key = recv_ref[:, :, columns(head, 1)].reshape(GROUP, HD)
        value = recv_ref[:, :, columns(head, 2)].reshape(GROUP, HD)
        scores = dot_nt(key, query) + bias
        top = jnp.max(scores, axis=0, keepdims=True)
        raised = jnp.exp2((scores - top) * (SCALE * LOG2E))
        inverse = live / jnp.sum(raised, axis=0, keepdims=True)
        weights = raised.astype(BF)
        raised_ref[head] = weights
        inverse_ref[head : head + 1, :] = inverse
        output = (dot_tn(value, weights) * inverse).astype(BF)
        for half in range(2):
            rows = dot_nt(order, output[:, half * 256 : (half + 1) * 256]).astype(BF)
            out_ref[:, pl.ds(half * 64, 64), pl.ds(head * HD, HD)] = rows.reshape(4, 64, HD)
    inverse_ref[HEADS_DEV:, :] = jnp.zeros((8 - HEADS_DEV, GROUP), F32)
    for step, ref in enumerate((o0_ref, o1_ref, o2_ref, o3_ref)):
        ref[...] = out_ref[jnp.bitwise_xor(mine, step)]


def backward_kernel(
    me_ref,
    recv_ref,
    raised_ref,
    inverse_ref,
    d0_ref,
    d1_ref,
    d2_ref,
    d3_ref,
    out_ref,
    cot_ref,
    grad_ref,
    ret_ref,
    out_sem,
):
    mine = me_ref[0] % N_SP
    for step, ref in enumerate((d0_ref, d1_ref, d2_ref, d3_ref)):
        cot_ref[jnp.bitwise_xor(mine, step)] = ref[...]
    order = quarters_first()
    for half in range(2):
        rows = cot_ref[:, pl.ds(half * 64, 64), :].reshape(256, PART)
        grad_ref[pl.ds(half * 256, 256), :] = dot_tn(order, rows).astype(BF)
    inverse_columns = inverse_ref[...].T
    stores = []
    for head in range(HEADS_DEV):
        query = recv_ref[:, :, columns(head, 0)].reshape(GROUP, HD)
        key = recv_ref[:, :, columns(head, 1)].reshape(GROUP, HD)
        value = recv_ref[:, :, columns(head, 2)].reshape(GROUP, HD)
        inverse = inverse_ref[head : head + 1, :]
        scale = inverse_columns[:, head : head + 1] * SCALE
        grad = (grad_ref[:, pl.ds(head * HD, HD)].astype(F32) * scale).astype(BF)
        weights = raised_ref[head]
        wide = weights.astype(F32)
        grad_attend = dot_nt(value, grad)
        row_dot = jnp.sum(wide * grad_attend, axis=0, keepdims=True) * inverse
        grad_scores = (wide * (grad_attend - row_dot)).astype(BF)
        grad_query = dot_tn(key, grad_scores).T.astype(BF)
        grad_key = dot(grad_scores, query).astype(BF)
        grad_value = (dot(weights, grad) * (1.0 / SCALE)).astype(BF)
        for array, result in enumerate((grad_query, grad_key, grad_value)):
            lanes = columns(head, array)
            ret_ref[:, :, lanes] = result.reshape(LOADERS, 4, HD)
            store = pltpu.make_async_copy(
                ret_ref.at[:, :, lanes], out_ref.at[:, :, lanes], out_sem.at[head, array]
            )
            store.start()
            stores.append(store)
    for store in stores:
        store.wait()


SMEM = pl.BlockSpec(memory_space=pltpu.SMEM)
VMEM = pl.BlockSpec(memory_space=pltpu.VMEM)
HBM = pl.BlockSpec(memory_space=pltpu.HBM)
PARAMS = pltpu.CompilerParams(vmem_limit_bytes=24 * 1024 * 1024)
AHEAD = pl.CostEstimate(flops=60_000_000_000, bytes_accessed=200_000_000, transcendentals=0)
PIECE = jax.ShapeDtypeStruct((ROWS, PART), BF)
WHOLE = jax.ShapeDtypeStruct((ROWS, WIDTH), BF)


def in_hbm(array):
    return pltpu.with_memory_space_constraint(array, pltpu.HBM)


def pack(me, table, queries, keys, values):
    chunks = pl.pallas_call(
        pack_kernel,
        out_shape=pltpu.HBM((N_DP, N_SP, 4, CHUNK), BF),
        in_specs=[SMEM] + [HBM] * 4,
        out_specs=HBM,
        scratch_shapes=[
            pltpu.VMEM((LOADERS, ROWS), jnp.int32),
            pltpu.VMEM((3, ROWS, WIDTH), BF),
            pltpu.VMEM((N_DP, N_SP, 4, CHUNK), BF),
            pltpu.SemaphoreType.DMA,
            pltpu.SemaphoreType.DMA((3,)),
            pltpu.SemaphoreType.DMA((3,)),
        ],
        compiler_params=PARAMS,
        name="pack",
    )(me, in_hbm(table), in_hbm(queries), in_hbm(keys), in_hbm(values))
    return chunks.reshape(LOADERS, 4, CHUNK)


def unpack(pick, chunks):
    return pl.pallas_call(
        unpack_kernel,
        out_shape=(pltpu.HBM((ROWS, WIDTH), BF),) * 3,
        in_specs=[VMEM] * 2,
        out_specs=(HBM,) * 3,
        scratch_shapes=[
            pltpu.VMEM((3, ROWS, WIDTH), BF),
            pltpu.SemaphoreType.DMA((3,)),
        ],
        compiler_params=PARAMS,
        name="unpack",
    )(pick, chunks.reshape(N_DP, N_SP, 4, CHUNK))


def spread(me, lengths, plan, bins, guide, table, cotangent):
    return pl.pallas_call(
        spread_kernel,
        out_shape=(PIECE,) * N_SP
        + (
            jax.ShapeDtypeStruct((GROUP, HD), F32),
            jax.ShapeDtypeStruct((8, GROUP), F32),
            jax.ShapeDtypeStruct((ROWS, LOADERS), BF),
        ),
        in_specs=[SMEM] * 5 + [VMEM] * 2,
        out_specs=(VMEM,) * (N_SP + 3),
        scratch_shapes=[pltpu.VMEM((ROWS, WIDTH), BF)],
        compiler_params=PARAMS,
        name="spread",
    )(me, lengths, plan, bins, guide, table, cotangent)


def collect(me, plan, bins, guide, table, pieces):
    return pl.pallas_call(
        collect_kernel,
        out_shape=WHOLE,
        in_specs=[SMEM] * 4 + [VMEM] * (1 + N_SP),
        out_specs=VMEM,
        compiler_params=PARAMS,
        cost_estimate=AHEAD,
        name="collect",
    )(me, plan, bins, guide, table, *pieces)


def forward(me, bias, live, chunks):
    return pl.pallas_call(
        forward_kernel,
        out_shape=(
            jax.ShapeDtypeStruct((HEADS_DEV, GROUP, GROUP), BF),
            jax.ShapeDtypeStruct((8, GROUP), F32),
        )
        + (PIECE,) * N_SP,
        in_specs=[SMEM] + [VMEM] * 3,
        out_specs=(VMEM,) * (2 + N_SP),
        scratch_shapes=[pltpu.VMEM((4, ROWS, PART), BF)],
        compiler_params=PARAMS,
        name="forward",
    )(me, bias, live, chunks)


def backward(me, chunks, raised, inverse, pieces):
    return pl.pallas_call(
        backward_kernel,
        out_shape=pltpu.HBM((LOADERS, 4, CHUNK), BF),
        in_specs=[SMEM] + [VMEM] * (3 + N_SP),
        out_specs=HBM,
        scratch_shapes=[
            pltpu.VMEM((4, ROWS, PART), BF),
            pltpu.VMEM((GROUP, PART), BF),
            pltpu.VMEM((LOADERS, 4, CHUNK), BF),
            pltpu.SemaphoreType.DMA((HEADS_DEV, 3)),
        ],
        compiler_params=PARAMS,
        name="backward",
    )(me, chunks, raised, inverse, *pieces)


def exchange(chunks):
    return lax.all_to_all(chunks, ("dp", "sp"), split_axis=0, concat_axis=0, tiled=True)


def swap_pieces(pieces):
    return [pieces[0]] + [
        lax.ppermute(pieces[step], "sp", [(i, i ^ step) for i in range(N_SP)]) for step in range(1, N_SP)
    ]


def per_device(
    queries,
    key_rows,
    value_rows,
    cotangent,
    lengths,
    sample_plan,
    guide_bins,
    guide_table,
    block_source,
):
    me = (lax.axis_index("dp") * N_SP + lax.axis_index("sp")).astype(jnp.int32).reshape(1)
    table = block_source.reshape(LOADERS, ROWS)
    chunks = exchange(pack(me, table, queries, key_rows, value_rows))
    *pieces, bias, live, pick = spread(
        me, lengths, sample_plan, guide_bins, guide_table, table, cotangent
    )
    chunks, pieces = lax.optimization_barrier((chunks, pieces))
    grad_pieces = swap_pieces(pieces)
    raised, inverse, *outs = forward(me, bias, live, chunks)
    out_pieces = swap_pieces(outs)
    grads = backward(me, chunks, raised, inverse, grad_pieces)
    back = exchange(grads)
    attn_out = collect(me, sample_plan, guide_bins, guide_table, table, out_pieces)
    return attn_out, *unpack(pick, back)


def solution(mesh):
    rows = P(("dp", "sp"), None)
    return jax.shard_map(
        per_device,
        mesh=mesh,
        in_specs=(rows,) * 4 + (P(),) * 5,
        out_specs=(rows,) * 4,
        check_vma=False,
    )
```

```python
import jax
import jax.numpy as jnp
from jax import lax
from jax.experimental import pallas as pl
from jax.experimental.pallas import tpu as pltpu
from jax.sharding import PartitionSpec as P

HEADS = 20
HD = 128
N_DP = 32
N_SP = 4
LOADERS = N_DP * N_SP
ROWS = 128
GROUP = 512
HEADS_DEV = HEADS // N_SP
WIDTH = HEADS * HD
PART = HEADS_DEV * HD
CHUNK = 3 * PART
SCALE = HD ** (-0.5)
LOG2E = 1.4426950408889634
BF = jnp.bfloat16
F32 = jnp.float32


def dot(a, b):
    return jnp.dot(a, b, preferred_element_type=F32)


def dot_nt(a, b):
    return lax.dot_general(a, b, (((1,), (1,)), ((), ())), preferred_element_type=F32)


def dot_tn(a, b):
    return lax.dot_general(a, b, (((0,), (0,)), ((), ())), preferred_element_type=F32)


def iota(shape, dim):
    return lax.broadcasted_iota(jnp.int32, shape, dim)


def onehot(hit):
    return jnp.where(hit, 1.0, 0.0).astype(BF)


def row_picker(table, me):
    slot = jnp.sum(jnp.where(table // ROWS == me, table % ROWS, 0), axis=1, keepdims=True)
    return onehot(slot == iota((LOADERS, ROWS), 1))


def quarters_first():
    row, col = iota((256, 256), 0), iota((256, 256), 1)
    return onehot(col == (row % 64) * 4 + row // 64)


def columns(head, array):
    return pl.ds((array * HEADS_DEV + head) * HD, HD)


def part_lanes(index):
    return pl.ds(pl.multiple_of(index * PART, HD), PART)


def sample_of(group, plan_ref, value_ref):
    value = jnp.int32(0)
    for sample in range(N_DP):
        value = jnp.where(plan_ref[sample] == group, value_ref[sample], value)
    return value


def pack_kernel(
    me_ref,
    table_ref,
    q_ref,
    k_ref,
    v_ref,
    cot_ref,
    out_ref,
    p0_ref,
    p1_ref,
    p2_ref,
    p3_ref,
    index_ref,
    in_ref,
    send_ref,
    index_sem,
    in_sem,
    out_sem,
    piece_sem,
):
    index = pltpu.make_async_copy(table_ref, index_ref, index_sem)
    index.start()
    loads = []
    for array, ref in enumerate((q_ref, k_ref, v_ref)):
        load = pltpu.make_async_copy(ref, in_ref.at[array], in_sem.at[array])
        load.start()
        loads.append(load)
    pieces = []
    for step, ref in enumerate((p0_ref, p1_ref, p2_ref, p3_ref)):
        lanes = part_lanes(jnp.bitwise_xor(me_ref[0] % N_SP, step))
        piece = pltpu.make_async_copy(cot_ref.at[:, lanes], ref, piece_sem.at[step])
        piece.start()
        pieces.append(piece)
    index.wait()
    pick = row_picker(index_ref[...], me_ref[0])
    stores = []
    for array in range(3):
        loads[array].wait()
        lanes = pl.ds(array * PART, PART)
        for part in range(N_SP):
            rows = dot(pick, in_ref[array, :, pl.ds(part * PART, PART)]).astype(BF)
            send_ref[:, part, :, lanes] = rows.reshape(N_DP, 4, PART)
        store = pltpu.make_async_copy(
            send_ref.at[:, :, :, lanes], out_ref.at[:, :, :, lanes], out_sem.at[array]
        )
        store.start()
        stores.append(store)
    for piece in pieces:
        piece.wait()
    for store in stores:
        store.wait()


def unpack_kernel(pick_ref, recv_ref, q_ref, k_ref, v_ref, out_ref, out_sem):
    pick = pick_ref[...]
    stores = []
    for array, ref in enumerate((q_ref, k_ref, v_ref)):
        for part in range(N_SP):
            rows = recv_ref[:, part, :, pl.ds(array * PART, PART)].reshape(ROWS, PART)
            out_ref[array, :, pl.ds(part * PART, PART)] = dot(pick, rows).astype(BF)
        store = pltpu.make_async_copy(out_ref.at[array], ref, out_sem.at[array])
        store.start()
        stores.append(store)
    for store in stores:
        store.wait()


def prepare_kernel(
    me_ref,
    lengths_ref,
    plan_ref,
    bins_ref,
    guide_ref,
    table_ref,
    d0_ref,
    d1_ref,
    d2_ref,
    d3_ref,
    grad_ref,
    bias_ref,
    live_ref,
    pick_ref,
    gated_ref,
    rows_ref,
):
    me = me_ref[0]
    group, mine = me // N_SP, me % N_SP
    group_len = sample_of(group, plan_ref, lengths_ref)
    group_bin = sample_of(group, plan_ref, bins_ref)
    for step, ref in enumerate((d0_ref, d1_ref, d2_ref, d3_ref)):
        for head in range(HEADS_DEV):
            lanes = pl.ds(head * HD, HD)
            gate = guide_ref[group_bin, mine * HEADS_DEV + head]
            gated_ref[jnp.bitwise_xor(mine, step), :, lanes] = (gate * ref[:, lanes].astype(F32)).astype(BF)
    for quarter in range(4):
        own = table_ref[pl.ds(group * N_SP + quarter, 1), :] // ROWS
        rows_ref[quarter] = dot(onehot(own == iota((LOADERS, ROWS), 0)), gated_ref[quarter]).astype(BF)
    order = quarters_first()
    for half in range(2):
        rows = rows_ref[:, pl.ds(half * 64, 64), :].reshape(256, PART)
        grad_ref[pl.ds(half * 256, 256), :] = dot_tn(order, rows).astype(BF)
    pick_ref[...] = row_picker(table_ref[...], me).astype(F32).T.astype(BF)
    row = iota((GROUP, ROWS), 0)
    source = jnp.zeros((GROUP, ROWS), jnp.int32)
    for quarter in range(4):
        own = table_ref[pl.ds(group * N_SP + quarter, 1), :] // ROWS
        source = jnp.where(row % 4 == quarter, own, source)
    place = onehot(source == row // 4)
    count = iota((ROWS, HD), 0).astype(F32).astype(BF)
    place_col = dot(place, count) + (ROWS * (row % 4)).astype(F32)
    bias_ref[...] = jnp.where(place_col < group_len.astype(F32), 0.0, -1e30)
    lane = iota((8, GROUP), 1)
    place_row = dot_nt(iota((8, ROWS), 1).astype(F32).astype(BF), place) + (ROWS * (lane % 4)).astype(F32)
    live_ref[...] = jnp.where(place_row < group_len.astype(F32), 1.0, 0.0)


def collect_kernel(me_ref, plan_ref, bins_ref, guide_ref, table_ref, i0_ref, i1_ref, i2_ref, i3_ref, out_ref):
    me = me_ref[0]
    group, mine = me // N_SP, me % N_SP
    group_bin = sample_of(group, plan_ref, bins_ref)
    order = onehot(table_ref[pl.ds(me, 1), :] // ROWS == iota((LOADERS, ROWS), 0)).astype(F32).T.astype(BF)
    for step, ref in enumerate((i0_ref, i1_ref, i2_ref, i3_ref)):
        out_ref[:, part_lanes(jnp.bitwise_xor(mine, step))] = dot(order, ref[...]).astype(BF)
    for head in range(HEADS):
        lanes = pl.ds(head * HD, HD)
        out_ref[:, lanes] = (guide_ref[group_bin, head] * out_ref[:, lanes].astype(F32)).astype(BF)


def forward_kernel(
    me_ref, bias_ref, live_ref, recv_ref, raised_ref, inverse_ref, o0_ref, o1_ref, o2_ref, o3_ref, out_ref
):
    mine = me_ref[0] % N_SP
    live = live_ref[0:1, :]
    bias = bias_ref[:, 0:1]
    for head in range(HEADS_DEV):
        query = recv_ref[:, :, columns(head, 0)].reshape(GROUP, HD)
        key = recv_ref[:, :, columns(head, 1)].reshape(GROUP, HD)
        value = recv_ref[:, :, columns(head, 2)].reshape(GROUP, HD)
        scores = dot_nt(key, query) + bias
        top = jnp.max(scores, axis=0, keepdims=True)
        raised = jnp.exp2((scores - top) * (SCALE * LOG2E))
        inverse = live / jnp.sum(raised, axis=0, keepdims=True)
        weights = raised.astype(BF)
        raised_ref[head] = weights
        inverse_ref[head : head + 1, :] = inverse
        output = dot_tn(value, weights) * inverse
        out_ref[:, pl.ds(head * HD, HD)] = output.T.astype(BF)
    inverse_ref[HEADS_DEV:, :] = jnp.zeros((8 - HEADS_DEV, GROUP), F32)
    for step, ref in enumerate((o0_ref, o1_ref, o2_ref, o3_ref)):
        quarter = onehot(iota((ROWS, GROUP), 1) == 4 * iota((ROWS, GROUP), 0) + jnp.bitwise_xor(mine, step))
        ref[...] = dot(quarter, out_ref[...]).astype(BF)


def backward_kernel(recv_ref, raised_ref, inverse_ref, grad_ref, out_ref, ret_ref, out_sem):
    inverse_columns = inverse_ref[...].T
    stores = []
    for head in range(HEADS_DEV):
        query = recv_ref[:, :, columns(head, 0)].reshape(GROUP, HD)
        key = recv_ref[:, :, columns(head, 1)].reshape(GROUP, HD)
        value = recv_ref[:, :, columns(head, 2)].reshape(GROUP, HD)
        inverse = inverse_ref[head : head + 1, :]
        scale = inverse_columns[:, head : head + 1] * SCALE
        grad = (grad_ref[:, pl.ds(head * HD, HD)].astype(F32) * scale).astype(BF)
        weights = raised_ref[head]
        wide = weights.astype(F32)
        grad_attend = dot_nt(value, grad)
        row_dot = jnp.sum(wide * grad_attend, axis=0, keepdims=True) * inverse
        grad_scores = (wide * (grad_attend - row_dot)).astype(BF)
        grad_query = dot_tn(key, grad_scores).T.astype(BF)
        grad_key = dot(grad_scores, query).astype(BF)
        grad_value = (dot(weights, grad) * (1.0 / SCALE)).astype(BF)
        for array, result in enumerate((grad_query, grad_key, grad_value)):
            lanes = columns(head, array)
            ret_ref[:, :, lanes] = result.reshape(LOADERS, 4, HD)
            store = pltpu.make_async_copy(
                ret_ref.at[:, :, lanes], out_ref.at[:, :, lanes], out_sem.at[head, array]
            )
            store.start()
            stores.append(store)
    for store in stores:
        store.wait()


SMEM = pl.BlockSpec(memory_space=pltpu.SMEM)
VMEM = pl.BlockSpec(memory_space=pltpu.VMEM)
HBM = pl.BlockSpec(memory_space=pltpu.HBM)
PARAMS = pltpu.CompilerParams(vmem_limit_bytes=24 * 1024 * 1024)
AHEAD = pl.CostEstimate(flops=60_000_000_000, bytes_accessed=200_000_000, transcendentals=0)
PIECE = jax.ShapeDtypeStruct((ROWS, PART), BF)
WHOLE = jax.ShapeDtypeStruct((ROWS, WIDTH), BF)


def in_hbm(array):
    return pltpu.with_memory_space_constraint(array, pltpu.HBM)


def pack(me, table, queries, keys, values, cotangent):
    chunks, *pieces = pl.pallas_call(
        pack_kernel,
        out_shape=(pltpu.HBM((N_DP, N_SP, 4, CHUNK), BF),) + (PIECE,) * N_SP,
        in_specs=[SMEM] + [HBM] * 5,
        out_specs=(HBM,) + (VMEM,) * N_SP,
        scratch_shapes=[
            pltpu.VMEM((LOADERS, ROWS), jnp.int32),
            pltpu.VMEM((3, ROWS, WIDTH), BF),
            pltpu.VMEM((N_DP, N_SP, 4, CHUNK), BF),
            pltpu.SemaphoreType.DMA,
            pltpu.SemaphoreType.DMA((3,)),
            pltpu.SemaphoreType.DMA((3,)),
            pltpu.SemaphoreType.DMA((N_SP,)),
        ],
        compiler_params=PARAMS,
        name="pack",
    )(me, in_hbm(table), in_hbm(queries), in_hbm(keys), in_hbm(values), in_hbm(cotangent))
    return chunks.reshape(LOADERS, 4, CHUNK), pieces


def unpack(pick, chunks):
    return pl.pallas_call(
        unpack_kernel,
        out_shape=(pltpu.HBM((ROWS, WIDTH), BF),) * 3,
        in_specs=[VMEM] * 2,
        out_specs=(HBM,) * 3,
        scratch_shapes=[
            pltpu.VMEM((3, ROWS, WIDTH), BF),
            pltpu.SemaphoreType.DMA((3,)),
        ],
        compiler_params=PARAMS,
        name="unpack",
    )(pick, chunks.reshape(N_DP, N_SP, 4, CHUNK))


def prepare(me, lengths, plan, bins, guide, table, pieces):
    return pl.pallas_call(
        prepare_kernel,
        out_shape=(
            jax.ShapeDtypeStruct((GROUP, PART), BF),
            jax.ShapeDtypeStruct((GROUP, HD), F32),
            jax.ShapeDtypeStruct((8, GROUP), F32),
            jax.ShapeDtypeStruct((ROWS, LOADERS), BF),
        ),
        in_specs=[SMEM] * 5 + [VMEM] * (1 + N_SP),
        out_specs=(VMEM,) * 4,
        scratch_shapes=[pltpu.VMEM((4, ROWS, PART), BF), pltpu.VMEM((4, ROWS, PART), BF)],
        compiler_params=PARAMS,
        cost_estimate=AHEAD,
        name="prepare",
    )(me, lengths, plan, bins, guide, table, *pieces)


def collect(me, plan, bins, guide, table, pieces):
    return pl.pallas_call(
        collect_kernel,
        out_shape=WHOLE,
        in_specs=[SMEM] * 4 + [VMEM] * (1 + N_SP),
        out_specs=VMEM,
        compiler_params=PARAMS,
        cost_estimate=AHEAD,
        name="collect",
    )(me, plan, bins, guide, table, *pieces)


def forward(me, bias, live, chunks):
    return pl.pallas_call(
        forward_kernel,
        out_shape=(
            jax.ShapeDtypeStruct((HEADS_DEV, GROUP, GROUP), BF),
            jax.ShapeDtypeStruct((8, GROUP), F32),
        )
        + (PIECE,) * N_SP,
        in_specs=[SMEM] + [VMEM] * 3,
        out_specs=(VMEM,) * (2 + N_SP),
        scratch_shapes=[pltpu.VMEM((GROUP, PART), BF)],
        compiler_params=PARAMS,
        name="forward",
    )(me, bias, live, chunks)


def backward(chunks, raised, inverse, grad):
    return pl.pallas_call(
        backward_kernel,
        out_shape=pltpu.HBM((LOADERS, 4, CHUNK), BF),
        in_specs=[VMEM] * 4,
        out_specs=HBM,
        scratch_shapes=[
            pltpu.VMEM((LOADERS, 4, CHUNK), BF),
            pltpu.SemaphoreType.DMA((HEADS_DEV, 3)),
        ],
        compiler_params=PARAMS,
        name="backward",
    )(chunks, raised, inverse, grad)


def exchange(chunks):
    return lax.all_to_all(chunks, ("dp", "sp"), split_axis=0, concat_axis=0, tiled=True)


def swap_pieces(pieces):
    return [pieces[0]] + [
        lax.ppermute(pieces[step], "sp", [(i, i ^ step) for i in range(N_SP)]) for step in range(1, N_SP)
    ]


def per_device(
    queries,
    key_rows,
    value_rows,
    cotangent,
    lengths,
    sample_plan,
    guide_bins,
    guide_table,
    block_source,
):
    me = (lax.axis_index("dp") * N_SP + lax.axis_index("sp")).astype(jnp.int32).reshape(1)
    table = block_source.reshape(LOADERS, ROWS)
    packed, pieces = pack(me, table, queries, key_rows, value_rows, cotangent)
    chunks = exchange(packed)
    grad, bias, live, pick = prepare(
        me, lengths, sample_plan, guide_bins, guide_table, table, swap_pieces(pieces)
    )
    raised, inverse, *outs = forward(me, bias, live, chunks)
    out_pieces = swap_pieces(outs)
    grads = backward(chunks, raised, inverse, grad)
    back = exchange(grads)
    attn_out = collect(me, sample_plan, guide_bins, guide_table, table, out_pieces)
    return attn_out, *unpack(pick, back)


def solution(mesh):
    rows = P(("dp", "sp"), None)
    return jax.shard_map(
        per_device,
        mesh=mesh,
        in_specs=(rows,) * 4 + (P(),) * 5,
        out_specs=(rows,) * 4,
        check_vma=False,
    )
```

```python
import jax
import jax.numpy as jnp
from jax import lax
from jax.experimental import pallas as pl
from jax.experimental.pallas import tpu as pltpu
from jax.sharding import PartitionSpec as P

HEADS = 20
HD = 128
N_DP = 32
N_SP = 4
LOADERS = N_DP * N_SP
ROWS = 128
GROUP = 512
HEADS_DEV = HEADS // N_SP
WIDTH = HEADS * HD
PART = HEADS_DEV * HD
CHUNK = 3 * PART
SCALE = HD ** (-0.5)
LOG2E = 1.4426950408889634
BF = jnp.bfloat16
F32 = jnp.float32


def dot(a, b):
    return jnp.dot(a, b, preferred_element_type=F32)


def dot_nt(a, b):
    return lax.dot_general(a, b, (((1,), (1,)), ((), ())), preferred_element_type=F32)


def dot_tn(a, b):
    return lax.dot_general(a, b, (((0,), (0,)), ((), ())), preferred_element_type=F32)


def iota(shape, dim):
    return lax.broadcasted_iota(jnp.int32, shape, dim)


def onehot(hit):
    return jnp.where(hit, 1.0, 0.0).astype(BF)


def row_picker(table, me):
    slot = jnp.sum(jnp.where(table // ROWS == me, table % ROWS, 0), axis=1, keepdims=True)
    return onehot(slot == iota((LOADERS, ROWS), 1))


def quarters_first():
    row, col = iota((256, 256), 0), iota((256, 256), 1)
    return onehot(col == (row % 64) * 4 + row // 64)


def columns(head, array):
    return pl.ds((array * HEADS_DEV + head) * HD, HD)


def part_lanes(index):
    return pl.ds(pl.multiple_of(index * PART, HD), PART)


def sample_of(group, plan_ref, value_ref):
    value = jnp.int32(0)
    for sample in range(N_DP):
        value = jnp.where(plan_ref[sample] == group, value_ref[sample], value)
    return value


def pack_kernel(
    me_ref,
    table_ref,
    q_ref,
    k_ref,
    v_ref,
    cot_ref,
    out_ref,
    near_ref,
    far_ref,
    index_ref,
    in_ref,
    send_ref,
    stage_ref,
    index_sem,
    in_sem,
    out_sem,
    piece_sem,
    near_sem,
):
    index = pltpu.make_async_copy(table_ref, index_ref, index_sem)
    index.start()
    loads = []
    for array, ref in enumerate((q_ref, k_ref, v_ref)):
        load = pltpu.make_async_copy(ref, in_ref.at[array], in_sem.at[array])
        load.start()
        loads.append(load)
    pieces = []
    for step, ref in ((1, stage_ref), (2, far_ref.at[0]), (3, far_ref.at[1])):
        lanes = part_lanes(jnp.bitwise_xor(me_ref[0] % N_SP, step))
        piece = pltpu.make_async_copy(cot_ref.at[:, lanes], ref, piece_sem.at[step - 1])
        piece.start()
        pieces.append(piece)
    index.wait()
    pick = row_picker(index_ref[...], me_ref[0])
    stores = []
    for array in range(3):
        loads[array].wait()
        if array == 2:
            pieces[0].wait()
            near = pltpu.make_async_copy(stage_ref, near_ref, near_sem)
            near.start()
            stores.append(near)
        lanes = pl.ds(array * PART, PART)
        for part in range(N_SP):
            rows = dot(pick, in_ref[array, :, pl.ds(part * PART, PART)]).astype(BF)
            send_ref[:, part, :, lanes] = rows.reshape(N_DP, 4, PART)
            if part % 2 == 1:
                parts = pl.ds(part - 1, 2)
                store = pltpu.make_async_copy(
                    send_ref.at[:, parts, :, lanes], out_ref.at[:, parts, :, lanes], out_sem.at[array, part // 2]
                )
                store.start()
                stores.append(store)
    for piece in pieces[1:]:
        piece.wait()
    for store in stores:
        store.wait()


def unpack_kernel(pick_ref, recv_ref, q_ref, k_ref, v_ref, out_ref, out_sem):
    pick = pick_ref[...]
    stores = []
    for array, ref in enumerate((q_ref, k_ref, v_ref)):
        for part in range(N_SP):
            rows = recv_ref[:, part, :, pl.ds(array * PART, PART)].reshape(ROWS, PART)
            out_ref[array, :, pl.ds(part * PART, PART)] = dot(pick, rows).astype(BF)
            if part % 2 == 1:
                lanes = pl.ds((part - 1) * PART, 2 * PART)
                store = pltpu.make_async_copy(
                    out_ref.at[array, :, lanes], ref.at[:, lanes], out_sem.at[array, part // 2]
                )
                store.start()
                stores.append(store)
    for store in stores:
        store.wait()


def prepare_kernel(
    me_ref,
    lengths_ref,
    plan_ref,
    bins_ref,
    guide_ref,
    table_ref,
    cot_ref,
    near_ref,
    far_ref,
    relay_ref,
    grad_ref,
    turned_ref,
    bias_ref,
    live_ref,
    pick_ref,
    own_ref,
    gated_ref,
    rows_ref,
    own_sem,
):
    me = me_ref[0]
    group, mine = me // N_SP, me % N_SP
    own_load = pltpu.make_async_copy(cot_ref.at[:, part_lanes(mine)], own_ref, own_sem)
    own_load.start()
    group_len = sample_of(group, plan_ref, lengths_ref)
    group_bin = sample_of(group, plan_ref, bins_ref)
    own_load.wait()
    for step, ref in enumerate((own_ref, near_ref, far_ref.at[0], relay_ref.at[1])):
        for head in range(HEADS_DEV):
            lanes = pl.ds(head * HD, HD)
            gate = guide_ref[group_bin, mine * HEADS_DEV + head]
            gated_ref[jnp.bitwise_xor(mine, step), :, lanes] = (gate * ref[:, lanes].astype(F32)).astype(BF)
    for quarter in range(4):
        own = table_ref[pl.ds(group * N_SP + quarter, 1), :] // ROWS
        rows_ref[quarter] = dot(onehot(own == iota((LOADERS, ROWS), 0)), gated_ref[quarter]).astype(BF)
    order = quarters_first()
    for half in range(2):
        rows = rows_ref[:, pl.ds(half * 64, 64), :].reshape(256, PART)
        grad = dot_tn(order, rows)
        grad_ref[pl.ds(half * 256, 256), :] = grad.astype(BF)
        for head in range(HEADS_DEV):
            lanes = slice(head * HD, (head + 1) * HD)
            turned_ref[lanes, pl.ds(half * 256, 256)] = grad[:, lanes].T.astype(BF)
    pick_ref[...] = row_picker(table_ref[...], me).astype(F32).T.astype(BF)
    row = iota((GROUP, ROWS), 0)
    source = jnp.zeros((GROUP, ROWS), jnp.int32)
    for quarter in range(4):
        own = table_ref[pl.ds(group * N_SP + quarter, 1), :] // ROWS
        source = jnp.where(row % 4 == quarter, own, source)
    place = onehot(source == row // 4)
    count = iota((ROWS, HD), 0).astype(F32).astype(BF)
    place_col = dot(place, count) + (ROWS * (row % 4)).astype(F32)
    bias_ref[...] = jnp.where(place_col < group_len.astype(F32), 0.0, -1e30)
    lane = iota((8, GROUP), 1)
    place_row = dot_nt(iota((8, ROWS), 1).astype(F32).astype(BF), place) + (ROWS * (lane % 4)).astype(F32)
    live_ref[...] = jnp.where(place_row < group_len.astype(F32), 1.0, 0.0)


def collect_kernel(me_ref, plan_ref, bins_ref, guide_ref, table_ref, i0_ref, i1_ref, far_ref, relay_ref, out_ref):
    me = me_ref[0]
    group, mine = me // N_SP, me % N_SP
    group_bin = sample_of(group, plan_ref, bins_ref)
    order = onehot(table_ref[pl.ds(me, 1), :] // ROWS == iota((LOADERS, ROWS), 0)).astype(F32).T.astype(BF)
    for step, ref in enumerate((i0_ref, i1_ref, far_ref.at[0], relay_ref.at[1])):
        out_ref[:, part_lanes(jnp.bitwise_xor(mine, step))] = dot(order, ref[...]).astype(BF)
    for head in range(HEADS):
        lanes = pl.ds(head * HD, HD)
        out_ref[:, lanes] = (guide_ref[group_bin, head] * out_ref[:, lanes].astype(F32)).astype(BF)


def forward_kernel(
    me_ref,
    bias_ref,
    live_ref,
    turned_ref,
    recv_ref,
    raised_ref,
    stats_ref,
    own_ref,
    near_ref,
    far_ref,
    out_ref,
    piece_ref,
    piece_sem,
):
    mine = me_ref[0] % N_SP
    live = live_ref[0:1, :]
    bias = bias_ref[:, 0:1]

    def item(head, array):
        return recv_ref[:, :, columns(head, array)].reshape(GROUP, HD)

    def score(head):
        return dot_nt(item(head, 1), item(head, 0)) + bias

    def attend(head, weights, inverse):
        output = dot_tn(item(head, 2), weights) * inverse
        turned = turned_ref[pl.ds(head * HD, HD), :].astype(F32)
        stats_ref[8 + head : 9 + head, :] = jnp.sum(output * turned, axis=0, keepdims=True)
        out_ref[:, pl.ds(head * HD, HD)] = output.T.astype(BF)

    following = score(0)
    earlier = None
    for head in range(HEADS_DEV):
        scores = following
        if head + 1 < HEADS_DEV:
            following = score(head + 1)
        top = jnp.max(scores, axis=0, keepdims=True)
        raised = jnp.exp2((scores - top) * (SCALE * LOG2E))
        inverse = live / jnp.sum(raised, axis=0, keepdims=True)
        weights = raised.astype(BF)
        raised_ref[head] = weights
        stats_ref[head : head + 1, :] = inverse
        if earlier is not None:
            attend(*earlier)
        earlier = (head, weights, inverse)
    attend(*earlier)
    stats_ref[HEADS_DEV:8, :] = jnp.zeros((8 - HEADS_DEV, GROUP), F32)
    stores = []
    for step, ref in ((2, far_ref.at[0]), (3, far_ref.at[1]), (1, near_ref), (0, own_ref)):
        quarter = onehot(iota((ROWS, GROUP), 1) == 4 * iota((ROWS, GROUP), 0) + jnp.bitwise_xor(mine, step))
        piece_ref[step] = dot(quarter, out_ref[...]).astype(BF)
        store = pltpu.make_async_copy(piece_ref.at[step], ref, piece_sem.at[step])
        store.start()
        stores.append(store)
    for store in stores:
        store.wait()


def backward_kernel(recv_ref, raised_ref, stats_ref, grad_ref, out_ref, ret_ref, out_sem):
    inverse_columns = stats_ref[0:8, :].T
    halves = [(head, half) for head in range(HEADS_DEV) for half in range(2)]
    stores = []

    def item(head, array, half=None):
        loaders = pl.ds(0, LOADERS) if half is None else pl.ds(half * 64, 64)
        return recv_ref[loaders, :, columns(head, array)].reshape(-1, HD)

    def attended(head, half):
        return dot_nt(item(head, 2), grad_ref[pl.ds(half * 256, 256), pl.ds(head * HD, HD)])

    ahead = [attended(*halves[0]), attended(*halves[1])]
    for index, (head, half) in enumerate(halves):
        grad_attend = ahead.pop(0)
        if index + 2 < len(halves):
            ahead.append(attended(*halves[index + 2]))
        rows = slice(half * 256, (half + 1) * 256)
        weights = raised_ref[head, :, rows]
        inverse = stats_ref[head : head + 1, rows]
        row_dot = stats_ref[8 + head : 9 + head, rows]
        grad_scores = (weights.astype(F32) * (grad_attend - row_dot)).astype(BF)
        column = inverse_columns[rows, head : head + 1]
        query = (item(head, 0, half).astype(F32) * (column * SCALE)).astype(BF)
        grad = (grad_ref[rows, pl.ds(head * HD, HD)].astype(F32) * column).astype(BF)
        grad_query = (dot_tn(item(head, 1), grad_scores) * (inverse * SCALE)).T.astype(BF)
        ret_ref[pl.ds(half * 64, 64), :, columns(head, 0)] = grad_query.reshape(64, 4, HD)
        if half == 0:
            grad_key, grad_value = dot(grad_scores, query), dot(weights, grad)
            continue
        grad_key += dot(grad_scores, query)
        grad_value += dot(weights, grad)
        ret_ref[:, :, columns(head, 1)] = grad_key.astype(BF).reshape(LOADERS, 4, HD)
        ret_ref[:, :, columns(head, 2)] = grad_value.astype(BF).reshape(LOADERS, 4, HD)
        for array in range(3):
            lanes = columns(head, array)
            store = pltpu.make_async_copy(
                ret_ref.at[:, :, lanes], out_ref.at[:, :, lanes], out_sem.at[head, array]
            )
            store.start()
            stores.append(store)
    for store in stores:
        store.wait()


SMEM = pl.BlockSpec(memory_space=pltpu.SMEM)
VMEM = pl.BlockSpec(memory_space=pltpu.VMEM)
HBM = pl.BlockSpec(memory_space=pltpu.HBM)
PARAMS = pltpu.CompilerParams(vmem_limit_bytes=24 * 1024 * 1024)
AHEAD = pl.CostEstimate(flops=15_000_000_000, bytes_accessed=50_000_000, transcendentals=0)
PIECES = jax.ShapeDtypeStruct((2, ROWS, PART), BF)
WHOLE = jax.ShapeDtypeStruct((ROWS, WIDTH), BF)


def in_hbm(array):
    return pltpu.with_memory_space_constraint(array, pltpu.HBM)


def pack(me, table, queries, keys, values, cotangent):
    chunks, *pieces = pl.pallas_call(
        pack_kernel,
        out_shape=(pltpu.HBM((N_DP, N_SP, 4, CHUNK), BF), pltpu.HBM((ROWS, PART), BF), PIECES),
        in_specs=[SMEM] + [HBM] * 5,
        out_specs=(HBM, HBM, VMEM),
        scratch_shapes=[
            pltpu.VMEM((LOADERS, ROWS), jnp.int32),
            pltpu.VMEM((3, ROWS, WIDTH), BF),
            pltpu.VMEM((N_DP, N_SP, 4, CHUNK), BF),
            pltpu.VMEM((ROWS, PART), BF),
            pltpu.SemaphoreType.DMA,
            pltpu.SemaphoreType.DMA((3,)),
            pltpu.SemaphoreType.DMA((3, 2)),
            pltpu.SemaphoreType.DMA((N_SP - 1,)),
            pltpu.SemaphoreType.DMA,
        ],
        compiler_params=PARAMS,
        name="pack",
    )(me, in_hbm(table), in_hbm(queries), in_hbm(keys), in_hbm(values), in_hbm(cotangent))
    return chunks.reshape(LOADERS, 4, CHUNK), pieces


def unpack(pick, chunks):
    return pl.pallas_call(
        unpack_kernel,
        out_shape=(pltpu.HBM((ROWS, WIDTH), BF),) * 3,
        in_specs=[VMEM] * 2,
        out_specs=(HBM,) * 3,
        scratch_shapes=[
            pltpu.VMEM((3, ROWS, WIDTH), BF),
            pltpu.SemaphoreType.DMA((3, 2)),
        ],
        compiler_params=PARAMS,
        name="unpack",
    )(pick, chunks.reshape(N_DP, N_SP, 4, CHUNK))


def prepare(me, lengths, plan, bins, guide, table, cotangent, pieces):
    return pl.pallas_call(
        prepare_kernel,
        out_shape=(
            jax.ShapeDtypeStruct((GROUP, PART), BF),
            jax.ShapeDtypeStruct((PART, GROUP), BF),
            jax.ShapeDtypeStruct((GROUP, HD), F32),
            jax.ShapeDtypeStruct((8, GROUP), F32),
            jax.ShapeDtypeStruct((ROWS, LOADERS), BF),
        ),
        in_specs=[SMEM] * 5 + [VMEM, HBM] + [VMEM] * 3,
        out_specs=(VMEM,) * 5,
        scratch_shapes=[
            pltpu.VMEM((ROWS, PART), BF),
            pltpu.VMEM((4, ROWS, PART), BF),
            pltpu.VMEM((4, ROWS, PART), BF),
            pltpu.SemaphoreType.DMA,
        ],
        compiler_params=PARAMS,
        cost_estimate=AHEAD,
        name="prepare",
    )(me, lengths, plan, bins, guide, table, in_hbm(cotangent), *pieces)


def collect(me, plan, bins, guide, table, pieces):
    return pl.pallas_call(
        collect_kernel,
        out_shape=WHOLE,
        in_specs=[SMEM] * 4 + [VMEM] * (1 + N_SP),
        out_specs=VMEM,
        compiler_params=PARAMS,
        cost_estimate=AHEAD,
        name="collect",
    )(me, plan, bins, guide, table, *pieces)


def forward(me, bias, live, turned, chunks):
    return pl.pallas_call(
        forward_kernel,
        out_shape=(
            jax.ShapeDtypeStruct((HEADS_DEV, GROUP, GROUP), BF),
            jax.ShapeDtypeStruct((16, GROUP), F32),
            pltpu.HBM((ROWS, PART), BF),
            pltpu.HBM((ROWS, PART), BF),
            pltpu.HBM((2, ROWS, PART), BF),
        ),
        in_specs=[SMEM] + [VMEM] * 4,
        out_specs=(VMEM, VMEM, HBM, HBM, HBM),
        scratch_shapes=[
            pltpu.VMEM((GROUP, PART), BF),
            pltpu.VMEM((N_SP, ROWS, PART), BF),
            pltpu.SemaphoreType.DMA((N_SP,)),
        ],
        compiler_params=PARAMS,
        name="forward",
    )(me, bias, live, turned, chunks)


def backward(chunks, raised, stats, grad):
    return pl.pallas_call(
        backward_kernel,
        out_shape=pltpu.HBM((LOADERS, 4, CHUNK), BF),
        in_specs=[VMEM] * 4,
        out_specs=HBM,
        scratch_shapes=[
            pltpu.VMEM((LOADERS, 4, CHUNK), BF),
            pltpu.SemaphoreType.DMA((HEADS_DEV, 3)),
        ],
        compiler_params=PARAMS,
        name="backward",
    )(chunks, raised, stats, grad)


def exchange(chunks):
    return lax.all_to_all(chunks, ("dp", "sp"), split_axis=0, concat_axis=0, tiled=True)


def swap(piece, step):
    return lax.ppermute(piece, "sp", [(i, i ^ step) for i in range(N_SP)])


def swap_pieces(near, far):
    far = swap(far, 2)
    return swap(near, 1), far, swap(far, 1)


def per_device(
    queries,
    key_rows,
    value_rows,
    cotangent,
    lengths,
    sample_plan,
    guide_bins,
    guide_table,
    block_source,
):
    me = (lax.axis_index("dp") * N_SP + lax.axis_index("sp")).astype(jnp.int32).reshape(1)
    table = block_source.reshape(LOADERS, ROWS)
    packed, pieces = pack(me, table, queries, key_rows, value_rows, cotangent)
    chunks = exchange(packed)
    grad, turned, bias, live, pick = prepare(
        me, lengths, sample_plan, guide_bins, guide_table, table, cotangent, swap_pieces(*pieces)
    )
    raised, stats, own, *outs = forward(me, bias, live, turned, chunks)
    out_pieces = own, *swap_pieces(*outs)
    grads = backward(chunks, raised, stats, grad)
    back = exchange(grads)
    attn_out = collect(me, sample_plan, guide_bins, guide_table, table, out_pieces)
    return attn_out, *unpack(pick, back)


def solution(mesh):
    rows = P(("dp", "sp"), None)
    return jax.shard_map(
        per_device,
        mesh=mesh,
        in_specs=(rows,) * 4 + (P(),) * 5,
        out_specs=(rows,) * 4,
        check_vma=False,
    )
```

```python
import jax
import jax.numpy as jnp
from jax import lax
from jax.experimental import pallas as pl
from jax.experimental.pallas import tpu as pltpu
from jax.sharding import PartitionSpec as P

HEADS = 20
HD = 128
N_DP = 32
N_SP = 4
LOADERS = N_DP * N_SP
ROWS = 128
GROUP = 512
HEADS_DEV = HEADS // N_SP
WIDTH = HEADS * HD
PART = HEADS_DEV * HD
CHUNK = 3 * PART
SCALE = HD ** (-0.5)
LOG2E = 1.4426950408889634
BF = jnp.bfloat16
F32 = jnp.float32


def dot(a, b):
    return jnp.dot(a, b, preferred_element_type=F32)


def dot_nt(a, b):
    return lax.dot_general(a, b, (((1,), (1,)), ((), ())), preferred_element_type=F32)


def dot_tn(a, b):
    return lax.dot_general(a, b, (((0,), (0,)), ((), ())), preferred_element_type=F32)


def iota(shape, dim):
    return lax.broadcasted_iota(jnp.int32, shape, dim)


def onehot(hit):
    return jnp.where(hit, 1.0, 0.0).astype(BF)


def owner(source):
    return lax.shift_right_logical(source, 7)


def row_picker(table, me):
    slot = jnp.sum(jnp.where(owner(table) == me, table & (ROWS - 1), 0), axis=1, keepdims=True)
    return onehot(slot == iota((LOADERS, ROWS), 1))


def quarters_first():
    row, col = iota((256, 256), 0), iota((256, 256), 1)
    return onehot(col == (row % 64) * 4 + row // 64)


def columns(head, array):
    return pl.ds((array * HEADS_DEV + head) * HD, HD)


def part_lanes(index):
    return pl.ds(pl.multiple_of(index * PART, HD), PART)


def sample_of(group, plan_ref, value_ref):
    value = jnp.int32(0)
    for sample in range(N_DP):
        value = jnp.where(plan_ref[sample] == group, value_ref[sample], value)
    return value


def pack_kernel(
    me_ref,
    table_ref,
    q_ref,
    k_ref,
    v_ref,
    cot_ref,
    out_ref,
    near_ref,
    far_ref,
    index_ref,
    in_ref,
    send_ref,
    stage_ref,
    index_sem,
    in_sem,
    out_sem,
    piece_sem,
    near_sem,
):
    index = pltpu.make_async_copy(table_ref, index_ref, index_sem)
    index.start()
    loads = []
    for array, ref in enumerate((q_ref, k_ref, v_ref)):
        load = pltpu.make_async_copy(ref, in_ref.at[array], in_sem.at[array])
        load.start()
        loads.append(load)
    pieces = []
    for step, ref in ((1, stage_ref), (2, far_ref.at[0]), (3, far_ref.at[1])):
        lanes = part_lanes(jnp.bitwise_xor(me_ref[0] % N_SP, step))
        piece = pltpu.make_async_copy(cot_ref.at[:, lanes], ref, piece_sem.at[step - 1])
        piece.start()
        pieces.append(piece)
    index.wait()
    pick = row_picker(index_ref[...], me_ref[0])
    stores = []
    for array in range(3):
        loads[array].wait()
        if array == 2:
            pieces[0].wait()
            near = pltpu.make_async_copy(stage_ref, near_ref, near_sem)
            near.start()
            stores.append(near)
        lanes = pl.ds(array * PART, PART)
        for part in range(N_SP):
            rows = dot(pick, in_ref[array, :, pl.ds(part * PART, PART)]).astype(BF)
            send_ref[:, part, :, lanes] = rows.reshape(N_DP, 4, PART)
        store = pltpu.make_async_copy(
            send_ref.at[:, :, :, lanes], out_ref.at[:, :, :, lanes], out_sem.at[array]
        )
        store.start()
        stores.append(store)
    for piece in pieces[1:]:
        piece.wait()
    for store in stores:
        store.wait()


def unpack_kernel(pick_ref, recv_ref, q_ref, k_ref, v_ref, out_ref, out_sem):
    pick = pick_ref[...]
    stores = []
    for array, ref in enumerate((q_ref, k_ref, v_ref)):
        for part in range(N_SP):
            rows = recv_ref[:, part, :, pl.ds(array * PART, PART)].reshape(ROWS, PART)
            out_ref[array, :, pl.ds(part * PART, PART)] = dot(pick, rows).astype(BF)
            if part % 2 == 1:
                lanes = pl.ds((part - 1) * PART, 2 * PART)
                store = pltpu.make_async_copy(
                    out_ref.at[array, :, lanes], ref.at[:, lanes], out_sem.at[array, part // 2]
                )
                store.start()
                stores.append(store)
    for store in stores:
        store.wait()


def prepare_kernel(
    me_ref,
    lengths_ref,
    plan_ref,
    bins_ref,
    guide_ref,
    table_ref,
    cot_ref,
    near_ref,
    far_ref,
    relay_ref,
    grad_ref,
    turned_ref,
    bias_ref,
    live_ref,
    pick_ref,
    own_ref,
    gated_ref,
    rows_ref,
    own_sem,
):
    me = me_ref[0]
    group, mine = me // N_SP, me % N_SP
    own_load = pltpu.make_async_copy(cot_ref.at[:, part_lanes(mine)], own_ref, own_sem)
    own_load.start()
    group_len = sample_of(group, plan_ref, lengths_ref)
    group_bin = sample_of(group, plan_ref, bins_ref)
    own_load.wait()
    for step, ref in enumerate((own_ref, near_ref, far_ref.at[0], relay_ref.at[1])):
        for head in range(HEADS_DEV):
            lanes = pl.ds(head * HD, HD)
            gate = guide_ref[group_bin, mine * HEADS_DEV + head]
            gated_ref[jnp.bitwise_xor(mine, step), :, lanes] = (gate * ref[:, lanes].astype(F32)).astype(BF)
    for quarter in range(4):
        own = owner(table_ref[pl.ds(group * N_SP + quarter, 1), :])
        rows_ref[quarter] = dot(onehot(own == iota((LOADERS, ROWS), 0)), gated_ref[quarter]).astype(BF)
    order = quarters_first()
    for half in range(2):
        rows = rows_ref[:, pl.ds(half * 64, 64), :].reshape(256, PART)
        grad = dot_tn(order, rows)
        grad_ref[pl.ds(half * 256, 256), :] = grad.astype(BF)
        for head in range(HEADS_DEV):
            lanes = slice(head * HD, (head + 1) * HD)
            turned_ref[lanes, pl.ds(half * 256, 256)] = grad[:, lanes].T.astype(BF)
    pick_ref[...] = row_picker(table_ref[...], me).astype(F32).T.astype(BF)
    row = iota((GROUP, ROWS), 0)
    source = jnp.zeros((GROUP, ROWS), jnp.int32)
    for quarter in range(4):
        own = owner(table_ref[pl.ds(group * N_SP + quarter, 1), :])
        source = jnp.where(row % 4 == quarter, own, source)
    place = onehot(source == row // 4)
    count = iota((ROWS, HD), 0).astype(F32).astype(BF)
    place_col = dot(place, count) + (ROWS * (row % 4)).astype(F32)
    bias_ref[...] = jnp.where(place_col < group_len.astype(F32), 0.0, -1e30)
    lane = iota((8, GROUP), 1)
    place_row = dot_nt(iota((8, ROWS), 1).astype(F32).astype(BF), place) + (ROWS * (lane % 4)).astype(F32)
    live_ref[...] = jnp.where(place_row < group_len.astype(F32), 1.0, 0.0)


def collect_kernel(me_ref, plan_ref, bins_ref, guide_ref, table_ref, i0_ref, i1_ref, far_ref, relay_ref, out_ref):
    me = me_ref[0]
    group, mine = me // N_SP, me % N_SP
    group_bin = sample_of(group, plan_ref, bins_ref)
    order = onehot(owner(table_ref[pl.ds(me, 1), :]) == iota((LOADERS, ROWS), 0)).astype(F32).T.astype(BF)
    for step, ref in enumerate((i0_ref, i1_ref, far_ref.at[0], relay_ref.at[1])):
        out_ref[:, part_lanes(jnp.bitwise_xor(mine, step))] = dot(order, ref[...]).astype(BF)
    for head in range(HEADS):
        lanes = pl.ds(head * HD, HD)
        out_ref[:, lanes] = (guide_ref[group_bin, head] * out_ref[:, lanes].astype(F32)).astype(BF)


def attend_kernel(
    me_ref,
    bias_ref,
    live_ref,
    grad_ref,
    turned_ref,
    recv_ref,
    out_ref,
    own_ref,
    near_ref,
    far_ref,
    rows_ref,
    piece_ref,
    raised_ref,
    stats_ref,
    ret_ref,
    piece_sem,
    out_sem,
):
    mine = me_ref[0] % N_SP
    live = live_ref[0:1, :]
    bias = bias_ref[:, 0:1]

    def item(head, array):
        return recv_ref[:, :, columns(head, array)].reshape(GROUP, HD)

    def score(head):
        return dot_nt(item(head, 1), item(head, 0)) + bias

    def attend(head, weights, inverse):
        output = dot_tn(item(head, 2), weights) * inverse
        turned = turned_ref[pl.ds(head * HD, HD), :].astype(F32)
        stats_ref[8 + head : 9 + head, :] = jnp.sum(output * turned, axis=0, keepdims=True)
        rows_ref[:, pl.ds(head * HD, HD)] = output.T.astype(BF)

    following = score(0)
    earlier = None
    for head in range(HEADS_DEV):
        scores = following
        if head + 1 < HEADS_DEV:
            following = score(head + 1)
        top = jnp.max(scores, axis=0, keepdims=True)
        raised = jnp.exp2((scores - top) * (SCALE * LOG2E))
        inverse = live / jnp.sum(raised, axis=0, keepdims=True)
        weights = raised.astype(BF)
        raised_ref[head] = weights
        stats_ref[head : head + 1, :] = inverse
        if earlier is not None:
            attend(*earlier)
        earlier = (head, weights, inverse)
    attend(*earlier)
    stats_ref[HEADS_DEV:8, :] = jnp.zeros((8 - HEADS_DEV, GROUP), F32)
    stores = []
    for step, ref in ((2, far_ref.at[0]), (3, far_ref.at[1]), (1, near_ref), (0, own_ref)):
        quarter = onehot(iota((ROWS, GROUP), 1) == 4 * iota((ROWS, GROUP), 0) + jnp.bitwise_xor(mine, step))
        piece_ref[step] = dot(quarter, rows_ref[...]).astype(BF)
        store = pltpu.make_async_copy(piece_ref.at[step], ref, piece_sem.at[step])
        store.start()
        stores.append(store)
    inverse_columns = stats_ref[0:8, :].T
    halves = [(head, half) for head in range(HEADS_DEV) for half in range(2)]
    def part_item(head, array, half=None):
        loaders = pl.ds(0, LOADERS) if half is None else pl.ds(half * 64, 64)
        return recv_ref[loaders, :, columns(head, array)].reshape(-1, HD)

    def attended(head, half):
        return dot_nt(part_item(head, 2), grad_ref[pl.ds(half * 256, 256), pl.ds(head * HD, HD)])

    ahead = [attended(*halves[0]), attended(*halves[1])]
    for index, (head, half) in enumerate(halves):
        grad_attend = ahead.pop(0)
        if index + 2 < len(halves):
            ahead.append(attended(*halves[index + 2]))
        rows = slice(half * 256, (half + 1) * 256)
        weights = raised_ref[head, :, rows]
        inverse = stats_ref[head : head + 1, rows]
        row_dot = stats_ref[8 + head : 9 + head, rows]
        grad_scores = (weights.astype(F32) * (grad_attend - row_dot)).astype(BF)
        column = inverse_columns[rows, head : head + 1]
        query = (part_item(head, 0, half).astype(F32) * (column * SCALE)).astype(BF)
        grad = (grad_ref[rows, pl.ds(head * HD, HD)].astype(F32) * column).astype(BF)
        grad_query = (dot_tn(part_item(head, 1), grad_scores) * (inverse * SCALE)).T.astype(BF)
        ret_ref[pl.ds(half * 64, 64), :, columns(head, 0)] = grad_query.reshape(64, 4, HD)
        if half == 0:
            grad_key, grad_value = dot(grad_scores, query), dot(weights, grad)
            continue
        grad_key += dot(grad_scores, query)
        grad_value += dot(weights, grad)
        ret_ref[:, :, columns(head, 1)] = grad_key.astype(BF).reshape(LOADERS, 4, HD)
        ret_ref[:, :, columns(head, 2)] = grad_value.astype(BF).reshape(LOADERS, 4, HD)
        for array in range(3):
            lanes = columns(head, array)
            store = pltpu.make_async_copy(
                ret_ref.at[:, :, lanes], out_ref.at[:, :, lanes], out_sem.at[head, array]
            )
            store.start()
            stores.append(store)
    for store in stores:
        store.wait()


SMEM = pl.BlockSpec(memory_space=pltpu.SMEM)
VMEM = pl.BlockSpec(memory_space=pltpu.VMEM)
HBM = pl.BlockSpec(memory_space=pltpu.HBM)
PARAMS = pltpu.CompilerParams(vmem_limit_bytes=24 * 1024 * 1024)
AHEAD = pl.CostEstimate(flops=15_000_000_000, bytes_accessed=50_000_000, transcendentals=0)
PIECES = jax.ShapeDtypeStruct((2, ROWS, PART), BF)
WHOLE = jax.ShapeDtypeStruct((ROWS, WIDTH), BF)


def in_hbm(array):
    return pltpu.with_memory_space_constraint(array, pltpu.HBM)


def pack(me, table, queries, keys, values, cotangent):
    chunks, *pieces = pl.pallas_call(
        pack_kernel,
        out_shape=(pltpu.HBM((N_DP, N_SP, 4, CHUNK), BF), pltpu.HBM((ROWS, PART), BF), PIECES),
        in_specs=[SMEM] + [HBM] * 5,
        out_specs=(HBM, HBM, VMEM),
        scratch_shapes=[
            pltpu.VMEM((LOADERS, ROWS), jnp.int32),
            pltpu.VMEM((3, ROWS, WIDTH), BF),
            pltpu.VMEM((N_DP, N_SP, 4, CHUNK), BF),
            pltpu.VMEM((ROWS, PART), BF),
            pltpu.SemaphoreType.DMA,
            pltpu.SemaphoreType.DMA((3,)),
            pltpu.SemaphoreType.DMA((3,)),
            pltpu.SemaphoreType.DMA((N_SP - 1,)),
            pltpu.SemaphoreType.DMA,
        ],
        compiler_params=PARAMS,
        name="pack",
    )(me, in_hbm(table), in_hbm(queries), in_hbm(keys), in_hbm(values), in_hbm(cotangent))
    return chunks.reshape(LOADERS, 4, CHUNK), pieces


def unpack(pick, chunks):
    return pl.pallas_call(
        unpack_kernel,
        out_shape=(pltpu.HBM((ROWS, WIDTH), BF),) * 3,
        in_specs=[VMEM] * 2,
        out_specs=(HBM,) * 3,
        scratch_shapes=[
            pltpu.VMEM((3, ROWS, WIDTH), BF),
            pltpu.SemaphoreType.DMA((3, 2)),
        ],
        compiler_params=PARAMS,
        name="unpack",
    )(pick, chunks.reshape(N_DP, N_SP, 4, CHUNK))


def prepare(me, lengths, plan, bins, guide, table, cotangent, pieces):
    return pl.pallas_call(
        prepare_kernel,
        out_shape=(
            jax.ShapeDtypeStruct((GROUP, PART), BF),
            jax.ShapeDtypeStruct((PART, GROUP), BF),
            jax.ShapeDtypeStruct((GROUP, HD), F32),
            jax.ShapeDtypeStruct((8, GROUP), F32),
            jax.ShapeDtypeStruct((ROWS, LOADERS), BF),
        ),
        in_specs=[SMEM] * 5 + [VMEM, HBM] + [VMEM] * 3,
        out_specs=(VMEM,) * 5,
        scratch_shapes=[
            pltpu.VMEM((ROWS, PART), BF),
            pltpu.VMEM((4, ROWS, PART), BF),
            pltpu.VMEM((4, ROWS, PART), BF),
            pltpu.SemaphoreType.DMA,
        ],
        compiler_params=PARAMS,
        cost_estimate=AHEAD,
        name="prepare",
    )(me, lengths, plan, bins, guide, table, in_hbm(cotangent), *pieces)


def collect(me, plan, bins, guide, table, pieces):
    return pl.pallas_call(
        collect_kernel,
        out_shape=WHOLE,
        in_specs=[SMEM] * 4 + [VMEM] * (1 + N_SP),
        out_specs=VMEM,
        compiler_params=PARAMS,
        cost_estimate=AHEAD,
        name="collect",
    )(me, plan, bins, guide, table, *pieces)


def attend(me, bias, live, grad, turned, chunks):
    return pl.pallas_call(
        attend_kernel,
        out_shape=(
            pltpu.HBM((LOADERS, 4, CHUNK), BF),
            pltpu.HBM((ROWS, PART), BF),
            pltpu.HBM((ROWS, PART), BF),
            pltpu.HBM((2, ROWS, PART), BF),
        ),
        in_specs=[SMEM] + [VMEM] * 5,
        out_specs=(HBM,) * 4,
        scratch_shapes=[
            pltpu.VMEM((GROUP, PART), BF),
            pltpu.VMEM((N_SP, ROWS, PART), BF),
            pltpu.VMEM((HEADS_DEV, GROUP, GROUP), BF),
            pltpu.VMEM((16, GROUP), F32),
            pltpu.VMEM((LOADERS, 4, CHUNK), BF),
            pltpu.SemaphoreType.DMA((N_SP,)),
            pltpu.SemaphoreType.DMA((HEADS_DEV, 3)),
        ],
        compiler_params=PARAMS,
        name="attend",
    )(me, bias, live, grad, turned, chunks)


def exchange(chunks):
    return lax.all_to_all(chunks, ("dp", "sp"), split_axis=0, concat_axis=0, tiled=True)


def swap(piece, step):
    return lax.ppermute(piece, "sp", [(i, i ^ step) for i in range(N_SP)])


def swap_pieces(near, far):
    far = swap(far, 2)
    return swap(near, 1), far, swap(far, 1)


def per_device(
    queries,
    key_rows,
    value_rows,
    cotangent,
    lengths,
    sample_plan,
    guide_bins,
    guide_table,
    block_source,
):
    me = (lax.axis_index("dp") * N_SP + lax.axis_index("sp")).astype(jnp.int32).reshape(1)
    table = block_source.reshape(LOADERS, ROWS)
    packed, pieces = pack(me, table, queries, key_rows, value_rows, cotangent)
    chunks = exchange(packed)
    grad, turned, bias, live, pick = prepare(
        me, lengths, sample_plan, guide_bins, guide_table, table, cotangent, swap_pieces(*pieces)
    )
    grads, own, *outs = attend(me, bias, live, grad, turned, chunks)
    out_pieces = own, *swap_pieces(*outs)
    back = exchange(grads)
    attn_out = collect(me, sample_plan, guide_bins, guide_table, table, out_pieces)
    return attn_out, *unpack(pick, back)


def solution(mesh):
    rows = P(("dp", "sp"), None)
    return jax.shard_map(
        per_device,
        mesh=mesh,
        in_specs=(rows,) * 4 + (P(),) * 5,
        out_specs=(rows,) * 4,
        check_vma=False,
    )
```

```python
import jax
import jax.numpy as jnp
from jax import lax
from jax.experimental import pallas as pl
from jax.experimental.pallas import tpu as pltpu
from jax.sharding import PartitionSpec as P

HEADS = 20
HD = 128
N_DP = 32
N_SP = 4
LOADERS = N_DP * N_SP
ROWS = 128
GROUP = 512
HEADS_DEV = HEADS // N_SP
WIDTH = HEADS * HD
PART = HEADS_DEV * HD
CHUNK = 3 * PART
SCALE = HD ** (-0.5)
LOG2E = 1.4426950408889634
BF = jnp.bfloat16
F32 = jnp.float32


def dot(a, b):
    return jnp.dot(a, b, preferred_element_type=F32)


def dot_nt(a, b):
    return lax.dot_general(a, b, (((1,), (1,)), ((), ())), preferred_element_type=F32)


def dot_tn(a, b):
    return lax.dot_general(a, b, (((0,), (0,)), ((), ())), preferred_element_type=F32)


def iota(shape, dim):
    return lax.broadcasted_iota(jnp.int32, shape, dim)


def onehot(hit):
    return jnp.where(hit, 1.0, 0.0).astype(BF)


def owner(source):
    return lax.shift_right_logical(source, 7)


def row_picker(table, me):
    slot = jnp.sum(jnp.where(owner(table) == me, table & (ROWS - 1), 0), axis=1, keepdims=True)
    return onehot(slot == iota((LOADERS, ROWS), 1))


def quarters_first():
    row, col = iota((256, 256), 0), iota((256, 256), 1)
    return onehot(col == (row % 64) * 4 + row // 64)


def columns(head, array):
    return pl.ds((array * HEADS_DEV + head) * HD, HD)


def part_lanes(index):
    return pl.ds(pl.multiple_of(index * PART, HD), PART)


def sample_of(group, plan_ref, value_ref):
    value = jnp.int32(0)
    for sample in range(N_DP):
        value = jnp.where(plan_ref[sample] == group, value_ref[sample], value)
    return value


def pack_kernel(
    me_ref,
    table_ref,
    q_ref,
    k_ref,
    v_ref,
    cot_ref,
    out_ref,
    near_ref,
    far_ref,
    index_ref,
    in_ref,
    send_ref,
    stage_ref,
    index_sem,
    in_sem,
    out_sem,
    piece_sem,
    near_sem,
):
    index = pltpu.make_async_copy(table_ref, index_ref, index_sem)
    index.start()
    loads = []
    for array, ref in enumerate((q_ref, k_ref, v_ref)):
        load = pltpu.make_async_copy(ref, in_ref.at[array], in_sem.at[array])
        load.start()
        loads.append(load)
    pieces = []
    for step, ref in ((1, stage_ref), (2, far_ref.at[0]), (3, far_ref.at[1])):
        lanes = part_lanes(jnp.bitwise_xor(me_ref[0] % N_SP, step))
        piece = pltpu.make_async_copy(cot_ref.at[:, lanes], ref, piece_sem.at[step - 1])
        piece.start(priority=1)
        pieces.append(piece)
    index.wait()
    pick = row_picker(index_ref[...], me_ref[0])
    stores = []
    for array in range(3):
        loads[array].wait()
        if array == 2:
            pieces[0].wait()
            near = pltpu.make_async_copy(stage_ref, near_ref, near_sem)
            near.start()
            stores.append(near)
        lanes = pl.ds(array * PART, PART)
        for part in range(N_SP):
            rows = dot(pick, in_ref[array, :, pl.ds(part * PART, PART)]).astype(BF)
            send_ref[:, part, :, lanes] = rows.reshape(N_DP, 4, PART)
        store = pltpu.make_async_copy(
            send_ref.at[:, :, :, lanes], out_ref.at[:, :, :, lanes], out_sem.at[array]
        )
        store.start(priority=1)
        stores.append(store)
    for piece in pieces[1:]:
        piece.wait()
    for store in stores:
        store.wait()


def unpack_kernel(pick_ref, recv_ref, q_ref, k_ref, v_ref, out_ref, out_sem):
    pick = pick_ref[...]
    stores = []
    for array, ref in enumerate((q_ref, k_ref, v_ref)):
        for part in range(N_SP):
            rows = recv_ref[:, part, :, pl.ds(array * PART, PART)].reshape(ROWS, PART)
            out_ref[array, :, pl.ds(part * PART, PART)] = dot(pick, rows).astype(BF)
            if part % 2 == 1:
                lanes = pl.ds((part - 1) * PART, 2 * PART)
                store = pltpu.make_async_copy(
                    out_ref.at[array, :, lanes], ref.at[:, lanes], out_sem.at[array, part // 2]
                )
                store.start()
                stores.append(store)
    for store in stores:
        store.wait()


def prepare_kernel(
    me_ref,
    lengths_ref,
    plan_ref,
    bins_ref,
    guide_ref,
    table_ref,
    cot_ref,
    near_ref,
    far_ref,
    relay_ref,
    grad_ref,
    turned_ref,
    bias_ref,
    live_ref,
    pick_ref,
    own_ref,
    gated_ref,
    rows_ref,
    own_sem,
):
    me = me_ref[0]
    group, mine = me // N_SP, me % N_SP
    own_load = pltpu.make_async_copy(cot_ref.at[:, part_lanes(mine)], own_ref, own_sem)
    own_load.start()
    group_len = sample_of(group, plan_ref, lengths_ref)
    group_bin = sample_of(group, plan_ref, bins_ref)
    own_load.wait()
    for step, ref in enumerate((own_ref, near_ref, far_ref.at[0], relay_ref.at[1])):
        for head in range(HEADS_DEV):
            lanes = pl.ds(head * HD, HD)
            gate = guide_ref[group_bin, mine * HEADS_DEV + head]
            gated_ref[jnp.bitwise_xor(mine, step), :, lanes] = (gate * ref[:, lanes].astype(F32)).astype(BF)
    for quarter in range(4):
        own = owner(table_ref[pl.ds(group * N_SP + quarter, 1), :])
        rows_ref[quarter] = dot(onehot(own == iota((LOADERS, ROWS), 0)), gated_ref[quarter]).astype(BF)
    order = quarters_first()
    for half in range(2):
        rows = rows_ref[:, pl.ds(half * 64, 64), :].reshape(256, PART)
        grad = dot_tn(order, rows)
        grad_ref[pl.ds(half * 256, 256), :] = grad.astype(BF)
        for head in range(HEADS_DEV):
            lanes = slice(head * HD, (head + 1) * HD)
            turned_ref[lanes, pl.ds(half * 256, 256)] = grad[:, lanes].T.astype(BF)
    pick_ref[...] = row_picker(table_ref[...], me).astype(F32).T.astype(BF)
    row = iota((GROUP, ROWS), 0)
    source = jnp.zeros((GROUP, ROWS), jnp.int32)
    for quarter in range(4):
        own = owner(table_ref[pl.ds(group * N_SP + quarter, 1), :])
        source = jnp.where(row % 4 == quarter, own, source)
    place = onehot(source == row // 4)
    count = iota((ROWS, HD), 0).astype(F32).astype(BF)
    place_col = dot(place, count) + (ROWS * (row % 4)).astype(F32)
    bias_ref[...] = jnp.where(place_col < group_len.astype(F32), 0.0, -1e30)
    lane = iota((8, GROUP), 1)
    place_row = dot_nt(iota((8, ROWS), 1).astype(F32).astype(BF), place) + (ROWS * (lane % 4)).astype(F32)
    live_ref[...] = jnp.where(place_row < group_len.astype(F32), 1.0, 0.0)


def collect_kernel(me_ref, plan_ref, bins_ref, guide_ref, table_ref, i0_ref, i1_ref, far_ref, relay_ref, out_ref):
    me = me_ref[0]
    group, mine = me // N_SP, me % N_SP
    group_bin = sample_of(group, plan_ref, bins_ref)
    order = onehot(owner(table_ref[pl.ds(me, 1), :]) == iota((LOADERS, ROWS), 0)).astype(F32).T.astype(BF)
    for step, ref in enumerate((i0_ref, i1_ref, far_ref.at[0], relay_ref.at[1])):
        out_ref[:, part_lanes(jnp.bitwise_xor(mine, step))] = dot(order, ref[...]).astype(BF)
    for head in range(HEADS):
        lanes = pl.ds(head * HD, HD)
        out_ref[:, lanes] = (guide_ref[group_bin, head] * out_ref[:, lanes].astype(F32)).astype(BF)


def attend_kernel(
    me_ref,
    bias_ref,
    live_ref,
    grad_ref,
    turned_ref,
    recv_ref,
    out_ref,
    own_ref,
    near_ref,
    far_ref,
    rows_ref,
    piece_ref,
    raised_ref,
    stats_ref,
    ret_ref,
    piece_sem,
    out_sem,
):
    mine = me_ref[0] % N_SP
    live = live_ref[0:1, :]
    bias = bias_ref[:, 0:1]

    def item(head, array):
        return recv_ref[:, :, columns(head, array)].reshape(GROUP, HD)

    def score(head):
        return dot_nt(item(head, 1), item(head, 0)) + bias

    def attend(head, weights, inverse):
        output = dot_tn(item(head, 2), weights) * inverse
        turned = turned_ref[pl.ds(head * HD, HD), :].astype(F32)
        stats_ref[8 + head : 9 + head, :] = jnp.sum(output * turned, axis=0, keepdims=True)
        rows_ref[:, pl.ds(head * HD, HD)] = output.T.astype(BF)

    following = score(0)
    earlier = None
    for head in range(HEADS_DEV):
        scores = following
        if head + 1 < HEADS_DEV:
            following = score(head + 1)
        top = jnp.max(scores, axis=0, keepdims=True)
        raised = jnp.exp2((scores - top) * (SCALE * LOG2E))
        inverse = live / jnp.sum(raised, axis=0, keepdims=True)
        weights = raised.astype(BF)
        raised_ref[head] = weights
        stats_ref[head : head + 1, :] = inverse
        if earlier is not None:
            attend(*earlier)
        earlier = (head, weights, inverse)
    attend(*earlier)
    stats_ref[HEADS_DEV:8, :] = jnp.zeros((8 - HEADS_DEV, GROUP), F32)
    stores = []
    for step, ref in ((2, far_ref.at[0]), (3, far_ref.at[1]), (1, near_ref), (0, own_ref)):
        quarter = onehot(iota((ROWS, GROUP), 1) == 4 * iota((ROWS, GROUP), 0) + jnp.bitwise_xor(mine, step))
        piece_ref[step] = dot(quarter, rows_ref[...]).astype(BF)
        store = pltpu.make_async_copy(piece_ref.at[step], ref, piece_sem.at[step])
        store.start()
        stores.append(store)
    inverse_columns = stats_ref[0:8, :].T
    halves = [(head, half) for head in range(HEADS_DEV) for half in range(2)]
    def part_item(head, array, half=None):
        loaders = pl.ds(0, LOADERS) if half is None else pl.ds(half * 64, 64)
        return recv_ref[loaders, :, columns(head, array)].reshape(-1, HD)

    def attended(head, half):
        return dot_nt(part_item(head, 2), grad_ref[pl.ds(half * 256, 256), pl.ds(head * HD, HD)])

    ahead = [attended(*halves[0]), attended(*halves[1])]
    for index, (head, half) in enumerate(halves):
        grad_attend = ahead.pop(0)
        if index + 2 < len(halves):
            ahead.append(attended(*halves[index + 2]))
        rows = slice(half * 256, (half + 1) * 256)
        weights = raised_ref[head, :, rows]
        inverse = stats_ref[head : head + 1, rows]
        row_dot = stats_ref[8 + head : 9 + head, rows]
        grad_scores = (weights.astype(F32) * (grad_attend - row_dot)).astype(BF)
        column = inverse_columns[rows, head : head + 1]
        query = (part_item(head, 0, half).astype(F32) * (column * SCALE)).astype(BF)
        grad = (grad_ref[rows, pl.ds(head * HD, HD)].astype(F32) * column).astype(BF)
        grad_query = (dot_tn(part_item(head, 1), grad_scores) * (inverse * SCALE)).T.astype(BF)
        ret_ref[pl.ds(half * 64, 64), :, columns(head, 0)] = grad_query.reshape(64, 4, HD)
        if half == 0:
            grad_key, grad_value = dot(grad_scores, query), dot(weights, grad)
            continue
        grad_key += dot(grad_scores, query)
        grad_value += dot(weights, grad)
        ret_ref[:, :, columns(head, 1)] = grad_key.astype(BF).reshape(LOADERS, 4, HD)
        ret_ref[:, :, columns(head, 2)] = grad_value.astype(BF).reshape(LOADERS, 4, HD)
        for array in range(3):
            lanes = columns(head, array)
            store = pltpu.make_async_copy(
                ret_ref.at[:, :, lanes], out_ref.at[:, :, lanes], out_sem.at[head, array]
            )
            store.start()
            stores.append(store)
    for store in stores:
        store.wait()


SMEM = pl.BlockSpec(memory_space=pltpu.SMEM)
VMEM = pl.BlockSpec(memory_space=pltpu.VMEM)
HBM = pl.BlockSpec(memory_space=pltpu.HBM)
PARAMS = pltpu.CompilerParams(vmem_limit_bytes=24 * 1024 * 1024)
AHEAD = pl.CostEstimate(flops=15_000_000_000, bytes_accessed=50_000_000, transcendentals=0)
PIECES = jax.ShapeDtypeStruct((2, ROWS, PART), BF)
WHOLE = jax.ShapeDtypeStruct((ROWS, WIDTH), BF)


def in_hbm(array):
    return pltpu.with_memory_space_constraint(array, pltpu.HBM)


def pack(me, table, queries, keys, values, cotangent):
    chunks, *pieces = pl.pallas_call(
        pack_kernel,
        out_shape=(pltpu.HBM((N_DP, N_SP, 4, CHUNK), BF), pltpu.HBM((ROWS, PART), BF), PIECES),
        in_specs=[SMEM] + [HBM] * 5,
        out_specs=(HBM, HBM, VMEM),
        scratch_shapes=[
            pltpu.VMEM((LOADERS, ROWS), jnp.int32),
            pltpu.VMEM((3, ROWS, WIDTH), BF),
            pltpu.VMEM((N_DP, N_SP, 4, CHUNK), BF),
            pltpu.VMEM((ROWS, PART), BF),
            pltpu.SemaphoreType.DMA,
            pltpu.SemaphoreType.DMA((3,)),
            pltpu.SemaphoreType.DMA((3,)),
            pltpu.SemaphoreType.DMA((N_SP - 1,)),
            pltpu.SemaphoreType.DMA,
        ],
        compiler_params=PARAMS,
        name="pack",
    )(me, in_hbm(table), in_hbm(queries), in_hbm(keys), in_hbm(values), in_hbm(cotangent))
    return chunks.reshape(LOADERS, 4, CHUNK), pieces


def unpack(pick, chunks):
    return pl.pallas_call(
        unpack_kernel,
        out_shape=(pltpu.HBM((ROWS, WIDTH), BF),) * 3,
        in_specs=[VMEM] * 2,
        out_specs=(HBM,) * 3,
        scratch_shapes=[
            pltpu.VMEM((3, ROWS, WIDTH), BF),
            pltpu.SemaphoreType.DMA((3, 2)),
        ],
        compiler_params=PARAMS,
        name="unpack",
    )(pick, chunks.reshape(N_DP, N_SP, 4, CHUNK))


def prepare(me, lengths, plan, bins, guide, table, cotangent, pieces):
    return pl.pallas_call(
        prepare_kernel,
        out_shape=(
            jax.ShapeDtypeStruct((GROUP, PART), BF),
            jax.ShapeDtypeStruct((PART, GROUP), BF),
            jax.ShapeDtypeStruct((GROUP, HD), F32),
            jax.ShapeDtypeStruct((8, GROUP), F32),
            jax.ShapeDtypeStruct((ROWS, LOADERS), BF),
        ),
        in_specs=[SMEM] * 5 + [VMEM, HBM] + [VMEM] * 3,
        out_specs=(VMEM,) * 5,
        scratch_shapes=[
            pltpu.VMEM((ROWS, PART), BF),
            pltpu.VMEM((4, ROWS, PART), BF),
            pltpu.VMEM((4, ROWS, PART), BF),
            pltpu.SemaphoreType.DMA,
        ],
        compiler_params=PARAMS,
        cost_estimate=AHEAD,
        name="prepare",
    )(me, lengths, plan, bins, guide, table, in_hbm(cotangent), *pieces)


def collect(me, plan, bins, guide, table, pieces):
    return pl.pallas_call(
        collect_kernel,
        out_shape=WHOLE,
        in_specs=[SMEM] * 4 + [VMEM] * (1 + N_SP),
        out_specs=VMEM,
        compiler_params=PARAMS,
        cost_estimate=AHEAD,
        name="collect",
    )(me, plan, bins, guide, table, *pieces)


def attend(me, bias, live, grad, turned, chunks):
    return pl.pallas_call(
        attend_kernel,
        out_shape=(
            pltpu.HBM((LOADERS, 4, CHUNK), BF),
            pltpu.HBM((ROWS, PART), BF),
            pltpu.HBM((ROWS, PART), BF),
            pltpu.HBM((2, ROWS, PART), BF),
        ),
        in_specs=[SMEM] + [VMEM] * 5,
        out_specs=(HBM,) * 4,
        scratch_shapes=[
            pltpu.VMEM((GROUP, PART), BF),
            pltpu.VMEM((N_SP, ROWS, PART), BF),
            pltpu.VMEM((HEADS_DEV, GROUP, GROUP), BF),
            pltpu.VMEM((16, GROUP), F32),
            pltpu.VMEM((LOADERS, 4, CHUNK), BF),
            pltpu.SemaphoreType.DMA((N_SP,)),
            pltpu.SemaphoreType.DMA((HEADS_DEV, 3)),
        ],
        compiler_params=PARAMS,
        name="attend",
    )(me, bias, live, grad, turned, chunks)


def exchange(chunks):
    return lax.all_to_all(chunks, ("dp", "sp"), split_axis=0, concat_axis=0, tiled=True)


def swap(piece, step):
    return lax.ppermute(piece, "sp", [(i, i ^ step) for i in range(N_SP)])


def swap_pieces(near, far):
    far = swap(far, 2)
    return swap(near, 1), far, swap(far, 1)


def per_device(
    queries,
    key_rows,
    value_rows,
    cotangent,
    lengths,
    sample_plan,
    guide_bins,
    guide_table,
    block_source,
):
    me = (lax.axis_index("dp") * N_SP + lax.axis_index("sp")).astype(jnp.int32).reshape(1)
    table = block_source.reshape(LOADERS, ROWS)
    packed, pieces = pack(me, table, queries, key_rows, value_rows, cotangent)
    chunks = exchange(packed)
    grad, turned, bias, live, pick = prepare(
        me, lengths, sample_plan, guide_bins, guide_table, table, cotangent, swap_pieces(*pieces)
    )
    grads, own, *outs = attend(me, bias, live, grad, turned, chunks)
    out_pieces = own, *swap_pieces(*outs)
    back = exchange(grads)
    attn_out = collect(me, sample_plan, guide_bins, guide_table, table, out_pieces)
    return attn_out, *unpack(pick, back)


def solution(mesh):
    rows = P(("dp", "sp"), None)
    return jax.shard_map(
        per_device,
        mesh=mesh,
        in_specs=(rows,) * 4 + (P(),) * 5,
        out_specs=(rows,) * 4,
        check_vma=False,
    )
```

```python
import jax
import jax.numpy as jnp
from jax import lax
from jax.experimental import pallas as pl
from jax.experimental.pallas import tpu as pltpu
from jax.sharding import PartitionSpec as P

HEADS = 20
HD = 128
N_DP = 32
N_SP = 4
LOADERS = N_DP * N_SP
ROWS = 128
GROUP = 512
HEADS_DEV = HEADS // N_SP
WIDTH = HEADS * HD
PART = HEADS_DEV * HD
CHUNK = 3 * PART
SCALE = HD ** (-0.5)
LOG2E = 1.4426950408889634
BF = jnp.bfloat16
F32 = jnp.float32


def dot(a, b):
    return jnp.dot(a, b, preferred_element_type=F32)


def dot_nt(a, b):
    return lax.dot_general(a, b, (((1,), (1,)), ((), ())), preferred_element_type=F32)


def dot_tn(a, b):
    return lax.dot_general(a, b, (((0,), (0,)), ((), ())), preferred_element_type=F32)


def iota(shape, dim):
    return lax.broadcasted_iota(jnp.int32, shape, dim)


def onehot(hit):
    return jnp.where(hit, 1.0, 0.0).astype(BF)


def owner(source):
    return lax.shift_right_logical(source, 7)


def row_picker(table, me):
    slot = jnp.sum(jnp.where(owner(table) == me, table & (ROWS - 1), 0), axis=1, keepdims=True)
    return onehot(slot == iota((LOADERS, ROWS), 1))


def quarters_first():
    row, col = iota((256, 256), 0), iota((256, 256), 1)
    return onehot(col == (row % 64) * 4 + row // 64)


def columns(head, array):
    return pl.ds((array * HEADS_DEV + head) * HD, HD)


def part_lanes(index):
    return pl.ds(pl.multiple_of(index * PART, HD), PART)


def sample_of(group, plan_ref, value_ref):
    value = jnp.int32(0)
    for sample in range(N_DP):
        value = jnp.where(plan_ref[sample] == group, value_ref[sample], value)
    return value


def pack_kernel(
    me_ref,
    table_ref,
    q_ref,
    k_ref,
    v_ref,
    cot_ref,
    out_ref,
    far_ref,
    index_ref,
    in_ref,
    send_ref,
    index_sem,
    in_sem,
    out_sem,
    piece_sem,
):
    index = pltpu.make_async_copy(table_ref, index_ref, index_sem)
    index.start()
    loads = []
    for array, ref in enumerate((q_ref, k_ref, v_ref)):
        load = pltpu.make_async_copy(ref, in_ref.at[array], in_sem.at[array])
        load.start()
        loads.append(load)
    pieces = []
    for step in (2, 3):
        lanes = part_lanes(jnp.bitwise_xor(me_ref[0] % N_SP, step))
        piece = pltpu.make_async_copy(cot_ref.at[:, lanes], far_ref.at[step - 2], piece_sem.at[step - 2])
        piece.start(priority=1)
        pieces.append(piece)
    index.wait()
    pick = row_picker(index_ref[...], me_ref[0])
    stores = []
    for array in range(3):
        loads[array].wait()
        lanes = pl.ds(array * PART, PART)
        for part in range(N_SP):
            rows = dot(pick, in_ref[array, :, pl.ds(part * PART, PART)]).astype(BF)
            send_ref[:, part, :, lanes] = rows.reshape(N_DP, 4, PART)
        store = pltpu.make_async_copy(
            send_ref.at[:, :, :, lanes], out_ref.at[:, :, :, lanes], out_sem.at[array]
        )
        store.start(priority=1)
        stores.append(store)
    for piece in pieces:
        piece.wait()
    for store in stores:
        store.wait()


def unpack_kernel(pick_ref, recv_ref, q_ref, k_ref, v_ref, out_ref, out_sem):
    pick = pick_ref[...]
    stores = []
    for array, ref in enumerate((q_ref, k_ref, v_ref)):
        for part in range(N_SP):
            rows = recv_ref[:, part, :, pl.ds(array * PART, PART)].reshape(ROWS, PART)
            out_ref[array, :, pl.ds(part * PART, PART)] = dot(pick, rows).astype(BF)
            if part % 2 == 1:
                lanes = pl.ds((part - 1) * PART, 2 * PART)
                store = pltpu.make_async_copy(
                    out_ref.at[array, :, lanes], ref.at[:, lanes], out_sem.at[array, part // 2]
                )
                store.start()
                stores.append(store)
    for store in stores:
        store.wait()


def prepare_kernel(
    me_ref,
    lengths_ref,
    plan_ref,
    bins_ref,
    guide_ref,
    table_ref,
    cot_ref,
    near_ref,
    far_ref,
    relay_ref,
    grad_ref,
    turned_ref,
    bias_ref,
    live_ref,
    pick_ref,
    own_ref,
    gated_ref,
    rows_ref,
    own_sem,
):
    me = me_ref[0]
    group, mine = me // N_SP, me % N_SP
    own_load = pltpu.make_async_copy(cot_ref.at[:, part_lanes(mine)], own_ref, own_sem)
    own_load.start()
    group_len = sample_of(group, plan_ref, lengths_ref)
    group_bin = sample_of(group, plan_ref, bins_ref)
    own_load.wait()
    for step, ref in enumerate((own_ref, near_ref, far_ref.at[0], relay_ref.at[1])):
        for head in range(HEADS_DEV):
            lanes = pl.ds(head * HD, HD)
            gate = guide_ref[group_bin, mine * HEADS_DEV + head]
            gated_ref[jnp.bitwise_xor(mine, step), :, lanes] = (gate * ref[:, lanes].astype(F32)).astype(BF)
    for quarter in range(4):
        own = owner(table_ref[pl.ds(group * N_SP + quarter, 1), :])
        rows_ref[quarter] = dot(onehot(own == iota((LOADERS, ROWS), 0)), gated_ref[quarter]).astype(BF)
    order = quarters_first()
    for half in range(2):
        rows = rows_ref[:, pl.ds(half * 64, 64), :].reshape(256, PART)
        grad = dot_tn(order, rows)
        grad_ref[pl.ds(half * 256, 256), :] = grad.astype(BF)
        for head in range(HEADS_DEV):
            lanes = slice(head * HD, (head + 1) * HD)
            turned_ref[lanes, pl.ds(half * 256, 256)] = grad[:, lanes].T.astype(BF)
    pick_ref[...] = row_picker(table_ref[...], me).astype(F32).T.astype(BF)
    row = iota((GROUP, ROWS), 0)
    source = jnp.zeros((GROUP, ROWS), jnp.int32)
    for quarter in range(4):
        own = owner(table_ref[pl.ds(group * N_SP + quarter, 1), :])
        source = jnp.where(row % 4 == quarter, own, source)
    place = onehot(source == row // 4)
    count = iota((ROWS, HD), 0).astype(F32).astype(BF)
    place_col = dot(place, count) + (ROWS * (row % 4)).astype(F32)
    bias_ref[...] = jnp.where(place_col < group_len.astype(F32), 0.0, -1e30)
    lane = iota((8, GROUP), 1)
    place_row = dot_nt(iota((8, ROWS), 1).astype(F32).astype(BF), place) + (ROWS * (lane % 4)).astype(F32)
    live_ref[...] = jnp.where(place_row < group_len.astype(F32), 1.0, 0.0)


def collect_kernel(me_ref, plan_ref, bins_ref, guide_ref, table_ref, i0_ref, i1_ref, far_ref, relay_ref, out_ref):
    me = me_ref[0]
    group, mine = me // N_SP, me % N_SP
    group_bin = sample_of(group, plan_ref, bins_ref)
    order = onehot(owner(table_ref[pl.ds(me, 1), :]) == iota((LOADERS, ROWS), 0)).astype(F32).T.astype(BF)
    for step, ref in enumerate((i0_ref, i1_ref, far_ref.at[0], relay_ref.at[1])):
        out_ref[:, part_lanes(jnp.bitwise_xor(mine, step))] = dot(order, ref[...]).astype(BF)
    for head in range(HEADS):
        lanes = pl.ds(head * HD, HD)
        out_ref[:, lanes] = (guide_ref[group_bin, head] * out_ref[:, lanes].astype(F32)).astype(BF)


def attend_kernel(
    me_ref,
    bias_ref,
    live_ref,
    grad_ref,
    turned_ref,
    recv_ref,
    out_ref,
    own_ref,
    near_ref,
    far_ref,
    rows_ref,
    piece_ref,
    raised_ref,
    stats_ref,
    ret_ref,
    piece_sem,
    out_sem,
):
    mine = me_ref[0] % N_SP
    live = live_ref[0:1, :]
    bias = bias_ref[:, 0:1]

    def item(head, array):
        return recv_ref[:, :, columns(head, array)].reshape(GROUP, HD)

    def score(head):
        return dot_nt(item(head, 1), item(head, 0)) + bias

    def attend(head, weights, inverse):
        output = dot_tn(item(head, 2), weights) * inverse
        turned = turned_ref[pl.ds(head * HD, HD), :].astype(F32)
        stats_ref[8 + head : 9 + head, :] = jnp.sum(output * turned, axis=0, keepdims=True)
        rows_ref[:, pl.ds(head * HD, HD)] = output.T.astype(BF)

    following = score(0)
    earlier = None
    for head in range(HEADS_DEV):
        scores = following
        if head + 1 < HEADS_DEV:
            following = score(head + 1)
        top = jnp.max(scores, axis=0, keepdims=True)
        raised = jnp.exp2((scores - top) * (SCALE * LOG2E))
        inverse = live / jnp.sum(raised, axis=0, keepdims=True)
        weights = raised.astype(BF)
        raised_ref[head] = weights
        stats_ref[head : head + 1, :] = inverse
        if earlier is not None:
            attend(*earlier)
        earlier = (head, weights, inverse)
    attend(*earlier)
    stats_ref[HEADS_DEV:8, :] = jnp.zeros((8 - HEADS_DEV, GROUP), F32)
    stores = []
    for step, ref in ((2, far_ref.at[0]), (3, far_ref.at[1]), (1, near_ref), (0, own_ref)):
        quarter = onehot(iota((ROWS, GROUP), 1) == 4 * iota((ROWS, GROUP), 0) + jnp.bitwise_xor(mine, step))
        piece_ref[step] = dot(quarter, rows_ref[...]).astype(BF)
        store = pltpu.make_async_copy(piece_ref.at[step], ref, piece_sem.at[step])
        store.start()
        stores.append(store)
    inverse_columns = stats_ref[0:8, :].T
    halves = [(head, half) for head in range(HEADS_DEV) for half in range(2)]
    def part_item(head, array, half=None):
        loaders = pl.ds(0, LOADERS) if half is None else pl.ds(half * 64, 64)
        return recv_ref[loaders, :, columns(head, array)].reshape(-1, HD)

    def attended(head, half):
        return dot_nt(part_item(head, 2), grad_ref[pl.ds(half * 256, 256), pl.ds(head * HD, HD)])

    ahead = [attended(*halves[0]), attended(*halves[1])]
    for index, (head, half) in enumerate(halves):
        grad_attend = ahead.pop(0)
        if index + 2 < len(halves):
            ahead.append(attended(*halves[index + 2]))
        rows = slice(half * 256, (half + 1) * 256)
        weights = raised_ref[head, :, rows]
        inverse = stats_ref[head : head + 1, rows]
        row_dot = stats_ref[8 + head : 9 + head, rows]
        grad_scores = (weights.astype(F32) * (grad_attend - row_dot)).astype(BF)
        column = inverse_columns[rows, head : head + 1]
        query = (part_item(head, 0, half).astype(F32) * (column * SCALE)).astype(BF)
        grad = (grad_ref[rows, pl.ds(head * HD, HD)].astype(F32) * column).astype(BF)
        grad_query = (dot_tn(part_item(head, 1), grad_scores) * (inverse * SCALE)).T.astype(BF)
        ret_ref[pl.ds(half * 64, 64), :, columns(head, 0)] = grad_query.reshape(64, 4, HD)
        if half == 0:
            grad_key, grad_value = dot(grad_scores, query), dot(weights, grad)
            continue
        grad_key += dot(grad_scores, query)
        grad_value += dot(weights, grad)
        ret_ref[:, :, columns(head, 1)] = grad_key.astype(BF).reshape(LOADERS, 4, HD)
        ret_ref[:, :, columns(head, 2)] = grad_value.astype(BF).reshape(LOADERS, 4, HD)
        for array in range(3):
            lanes = columns(head, array)
            store = pltpu.make_async_copy(
                ret_ref.at[:, :, lanes], out_ref.at[:, :, lanes], out_sem.at[head, array]
            )
            store.start()
            stores.append(store)
    for store in stores:
        store.wait()


SMEM = pl.BlockSpec(memory_space=pltpu.SMEM)
VMEM = pl.BlockSpec(memory_space=pltpu.VMEM)
HBM = pl.BlockSpec(memory_space=pltpu.HBM)
PARAMS = pltpu.CompilerParams(vmem_limit_bytes=24 * 1024 * 1024)
AHEAD = pl.CostEstimate(flops=15_000_000_000, bytes_accessed=50_000_000, transcendentals=0)
PIECES = jax.ShapeDtypeStruct((2, ROWS, PART), BF)
WHOLE = jax.ShapeDtypeStruct((ROWS, WIDTH), BF)


def in_hbm(array):
    return pltpu.with_memory_space_constraint(array, pltpu.HBM)


def pack(me, table, queries, keys, values, cotangent):
    chunks, far = pl.pallas_call(
        pack_kernel,
        out_shape=(pltpu.HBM((N_DP, N_SP, 4, CHUNK), BF), PIECES),
        in_specs=[SMEM] + [HBM] * 5,
        out_specs=(HBM, VMEM),
        scratch_shapes=[
            pltpu.VMEM((LOADERS, ROWS), jnp.int32),
            pltpu.VMEM((3, ROWS, WIDTH), BF),
            pltpu.VMEM((N_DP, N_SP, 4, CHUNK), BF),
            pltpu.SemaphoreType.DMA,
            pltpu.SemaphoreType.DMA((3,)),
            pltpu.SemaphoreType.DMA((3,)),
            pltpu.SemaphoreType.DMA((2,)),
        ],
        compiler_params=PARAMS,
        name="pack",
    )(me, in_hbm(table), in_hbm(queries), in_hbm(keys), in_hbm(values), in_hbm(cotangent))
    return chunks.reshape(LOADERS, 4, CHUNK), far


def unpack(pick, chunks):
    return pl.pallas_call(
        unpack_kernel,
        out_shape=(pltpu.HBM((ROWS, WIDTH), BF),) * 3,
        in_specs=[VMEM] * 2,
        out_specs=(HBM,) * 3,
        scratch_shapes=[
            pltpu.VMEM((3, ROWS, WIDTH), BF),
            pltpu.SemaphoreType.DMA((3, 2)),
        ],
        compiler_params=PARAMS,
        name="unpack",
    )(pick, chunks.reshape(N_DP, N_SP, 4, CHUNK))


def prepare(me, lengths, plan, bins, guide, table, cotangent, pieces):
    return pl.pallas_call(
        prepare_kernel,
        out_shape=(
            jax.ShapeDtypeStruct((GROUP, PART), BF),
            jax.ShapeDtypeStruct((PART, GROUP), BF),
            jax.ShapeDtypeStruct((GROUP, HD), F32),
            jax.ShapeDtypeStruct((8, GROUP), F32),
            jax.ShapeDtypeStruct((ROWS, LOADERS), BF),
        ),
        in_specs=[SMEM] * 5 + [VMEM, HBM] + [VMEM] * 3,
        out_specs=(VMEM,) * 5,
        scratch_shapes=[
            pltpu.VMEM((ROWS, PART), BF),
            pltpu.VMEM((4, ROWS, PART), BF),
            pltpu.VMEM((4, ROWS, PART), BF),
            pltpu.SemaphoreType.DMA,
        ],
        compiler_params=PARAMS,
        cost_estimate=AHEAD,
        name="prepare",
    )(me, lengths, plan, bins, guide, table, in_hbm(cotangent), *pieces)


def collect(me, plan, bins, guide, table, pieces):
    return pl.pallas_call(
        collect_kernel,
        out_shape=WHOLE,
        in_specs=[SMEM] * 4 + [VMEM] * (1 + N_SP),
        out_specs=VMEM,
        compiler_params=PARAMS,
        cost_estimate=AHEAD,
        name="collect",
    )(me, plan, bins, guide, table, *pieces)


def attend(me, bias, live, grad, turned, chunks):
    return pl.pallas_call(
        attend_kernel,
        out_shape=(
            pltpu.HBM((LOADERS, 4, CHUNK), BF),
            pltpu.HBM((ROWS, PART), BF),
            pltpu.HBM((ROWS, PART), BF),
            pltpu.HBM((2, ROWS, PART), BF),
        ),
        in_specs=[SMEM] + [VMEM] * 5,
        out_specs=(HBM,) * 4,
        scratch_shapes=[
            pltpu.VMEM((GROUP, PART), BF),
            pltpu.VMEM((N_SP, ROWS, PART), BF),
            pltpu.VMEM((HEADS_DEV, GROUP, GROUP), BF),
            pltpu.VMEM((16, GROUP), F32),
            pltpu.VMEM((LOADERS, 4, CHUNK), BF),
            pltpu.SemaphoreType.DMA((N_SP,)),
            pltpu.SemaphoreType.DMA((HEADS_DEV, 3)),
        ],
        compiler_params=PARAMS,
        name="attend",
    )(me, bias, live, grad, turned, chunks)


def exchange(chunks):
    return lax.all_to_all(chunks, ("dp", "sp"), split_axis=0, concat_axis=0, tiled=True)


def swap(piece, step):
    return lax.ppermute(piece, "sp", [(i, i ^ step) for i in range(N_SP)])


def swap_pieces(near, far):
    far = swap(far, 2)
    return swap(near, 1), far, swap(far, 1)


def per_device(
    queries,
    key_rows,
    value_rows,
    cotangent,
    lengths,
    sample_plan,
    guide_bins,
    guide_table,
    block_source,
):
    me = (lax.axis_index("dp") * N_SP + lax.axis_index("sp")).astype(jnp.int32).reshape(1)
    table = block_source.reshape(LOADERS, ROWS)
    packed, far = pack(me, table, queries, key_rows, value_rows, cotangent)
    chunks = exchange(packed)
    near = lax.dynamic_slice_in_dim(cotangent, jnp.bitwise_xor(lax.axis_index("sp"), 1) * PART, PART, axis=1)
    grad, turned, bias, live, pick = prepare(
        me, lengths, sample_plan, guide_bins, guide_table, table, cotangent, swap_pieces(near, far)
    )
    grads, own, *outs = attend(me, bias, live, grad, turned, chunks)
    out_pieces = own, *swap_pieces(*outs)
    back = exchange(grads)
    attn_out = collect(me, sample_plan, guide_bins, guide_table, table, out_pieces)
    return attn_out, *unpack(pick, back)


def solution(mesh):
    rows = P(("dp", "sp"), None)
    return jax.shard_map(
        per_device,
        mesh=mesh,
        in_specs=(rows,) * 4 + (P(),) * 5,
        out_specs=(rows,) * 4,
        check_vma=False,
    )
```

```python
import jax
import jax.numpy as jnp
from jax import lax
from jax.experimental import pallas as pl
from jax.experimental.pallas import tpu as pltpu
from jax.sharding import PartitionSpec as P

HEADS = 20
HD = 128
N_DP = 32
N_SP = 4
LOADERS = N_DP * N_SP
ROWS = 128
GROUP = 512
HEADS_DEV = HEADS // N_SP
WIDTH = HEADS * HD
PART = HEADS_DEV * HD
CHUNK = 3 * PART
SCALE = HD ** (-0.5)
LOG2E = 1.4426950408889634
BF = jnp.bfloat16
F32 = jnp.float32


def dot(a, b):
    return jnp.dot(a, b, preferred_element_type=F32)


def dot_nt(a, b):
    return lax.dot_general(a, b, (((1,), (1,)), ((), ())), preferred_element_type=F32)


def dot_tn(a, b):
    return lax.dot_general(a, b, (((0,), (0,)), ((), ())), preferred_element_type=F32)


def iota(shape, dim):
    return lax.broadcasted_iota(jnp.int32, shape, dim)


def onehot(hit):
    return jnp.where(hit, 1.0, 0.0).astype(BF)


def owner(source):
    return lax.shift_right_logical(source, 7)


def row_picker(table, me):
    slot = jnp.sum(jnp.where(owner(table) == me, table & (ROWS - 1), 0), axis=1, keepdims=True)
    return onehot(slot == iota((LOADERS, ROWS), 1))


def quarters_first():
    row, col = iota((256, 256), 0), iota((256, 256), 1)
    return onehot(col == (row % 64) * 4 + row // 64)


def columns(head, array):
    return pl.ds((array * HEADS_DEV + head) * HD, HD)


def part_lanes(index):
    return pl.ds(pl.multiple_of(index * PART, HD), PART)


def sample_of(group, plan_ref, value_ref):
    value = jnp.int32(0)
    for sample in range(N_DP):
        value = jnp.where(plan_ref[sample] == group, value_ref[sample], value)
    return value


def pack_kernel(
    me_ref,
    table_ref,
    q_ref,
    k_ref,
    v_ref,
    cot_ref,
    out_ref,
    far_ref,
    index_ref,
    in_ref,
    send_ref,
    index_sem,
    in_sem,
    out_sem,
    piece_sem,
):
    index = pltpu.make_async_copy(table_ref, index_ref, index_sem)
    index.start()
    loads = []
    for array, ref in enumerate((q_ref, k_ref, v_ref)):
        load = pltpu.make_async_copy(ref, in_ref.at[array], in_sem.at[array])
        load.start()
        loads.append(load)
    pieces = []
    for step in (2, 3):
        lanes = part_lanes(jnp.bitwise_xor(me_ref[0] % N_SP, step))
        piece = pltpu.make_async_copy(cot_ref.at[:, lanes], far_ref.at[step - 2], piece_sem.at[step - 2])
        piece.start(priority=1)
        pieces.append(piece)
    index.wait()
    pick = row_picker(index_ref[...], me_ref[0])
    stores = []
    for array in range(3):
        loads[array].wait()
        lanes = pl.ds(array * PART, PART)
        for part in range(N_SP):
            rows = dot(pick, in_ref[array, :, pl.ds(part * PART, PART)]).astype(BF)
            send_ref[:, part, :, lanes] = rows.reshape(N_DP, 4, PART)
        store = pltpu.make_async_copy(
            send_ref.at[:, :, :, lanes], out_ref.at[:, :, :, lanes], out_sem.at[array]
        )
        store.start(priority=1)
        stores.append(store)
    for piece in pieces:
        piece.wait()
    for store in stores:
        store.wait()


def unpack_kernel(pick_ref, recv_ref, q_ref, k_ref, v_ref, out_ref, out_sem):
    pick = pick_ref[...]
    stores = []
    for array, ref in enumerate((q_ref, k_ref, v_ref)):
        for part in range(N_SP):
            rows = recv_ref[:, part, :, pl.ds(array * PART, PART)].reshape(ROWS, PART)
            out_ref[array, :, pl.ds(part * PART, PART)] = dot(pick, rows).astype(BF)
            lanes = pl.ds(part * PART, PART)
            store = pltpu.make_async_copy(out_ref.at[array, :, lanes], ref.at[:, lanes], out_sem.at[array, part])
            store.start()
            stores.append(store)
    for store in stores:
        store.wait()


def prepare_kernel(
    me_ref,
    lengths_ref,
    plan_ref,
    bins_ref,
    guide_ref,
    table_ref,
    cot_ref,
    near_ref,
    far_ref,
    relay_ref,
    grad_ref,
    turned_ref,
    bias_ref,
    live_ref,
    pick_ref,
    own_ref,
    gated_ref,
    rows_ref,
    own_sem,
):
    me = me_ref[0]
    group, mine = me // N_SP, me % N_SP
    own_load = pltpu.make_async_copy(cot_ref.at[:, part_lanes(mine)], own_ref, own_sem)
    own_load.start()
    group_len = sample_of(group, plan_ref, lengths_ref)
    group_bin = sample_of(group, plan_ref, bins_ref)
    own_load.wait()
    for step, ref in enumerate((own_ref, near_ref, far_ref.at[0], relay_ref.at[1])):
        for head in range(HEADS_DEV):
            lanes = pl.ds(head * HD, HD)
            gate = guide_ref[group_bin, mine * HEADS_DEV + head]
            gated_ref[jnp.bitwise_xor(mine, step), :, lanes] = (gate * ref[:, lanes].astype(F32)).astype(BF)
    for quarter in range(4):
        own = owner(table_ref[pl.ds(group * N_SP + quarter, 1), :])
        rows_ref[quarter] = dot(onehot(own == iota((LOADERS, ROWS), 0)), gated_ref[quarter]).astype(BF)
    order = quarters_first()
    for half in range(2):
        rows = rows_ref[:, pl.ds(half * 64, 64), :].reshape(256, PART)
        grad = dot_tn(order, rows)
        grad_ref[pl.ds(half * 256, 256), :] = grad.astype(BF)
        for head in range(HEADS_DEV):
            lanes = slice(head * HD, (head + 1) * HD)
            turned_ref[lanes, pl.ds(half * 256, 256)] = grad[:, lanes].T.astype(BF)
    pick_ref[...] = row_picker(table_ref[...], me).astype(F32).T.astype(BF)
    row = iota((GROUP, ROWS), 0)
    source = jnp.zeros((GROUP, ROWS), jnp.int32)
    for quarter in range(4):
        own = owner(table_ref[pl.ds(group * N_SP + quarter, 1), :])
        source = jnp.where(row % 4 == quarter, own, source)
    place = onehot(source == row // 4)
    count = iota((ROWS, HD), 0).astype(F32).astype(BF)
    place_col = dot(place, count) + (ROWS * (row % 4)).astype(F32)
    bias_ref[...] = jnp.where(place_col < group_len.astype(F32), 0.0, -1e30)
    lane = iota((8, GROUP), 1)
    place_row = dot_nt(iota((8, ROWS), 1).astype(F32).astype(BF), place) + (ROWS * (lane % 4)).astype(F32)
    live_ref[...] = jnp.where(place_row < group_len.astype(F32), 1.0, 0.0)


def collect_kernel(me_ref, plan_ref, bins_ref, guide_ref, table_ref, i0_ref, i1_ref, far_ref, relay_ref, out_ref):
    me = me_ref[0]
    group, mine = me // N_SP, me % N_SP
    group_bin = sample_of(group, plan_ref, bins_ref)
    order = onehot(owner(table_ref[pl.ds(me, 1), :]) == iota((LOADERS, ROWS), 0)).astype(F32).T.astype(BF)
    for step, ref in enumerate((i0_ref, i1_ref, far_ref.at[0], relay_ref.at[1])):
        out_ref[:, part_lanes(jnp.bitwise_xor(mine, step))] = dot(order, ref[...]).astype(BF)
    for head in range(HEADS):
        lanes = pl.ds(head * HD, HD)
        out_ref[:, lanes] = (guide_ref[group_bin, head] * out_ref[:, lanes].astype(F32)).astype(BF)


def attend_kernel(
    me_ref,
    bias_ref,
    live_ref,
    grad_ref,
    turned_ref,
    recv_ref,
    out_ref,
    own_ref,
    near_ref,
    far_ref,
    rows_ref,
    piece_ref,
    raised_ref,
    stats_ref,
    ret_ref,
    piece_sem,
    out_sem,
):
    mine = me_ref[0] % N_SP
    live = live_ref[0:1, :]
    bias = bias_ref[:, 0:1]

    def item(head, array):
        return recv_ref[:, :, columns(head, array)].reshape(GROUP, HD)

    def score(head):
        return dot_nt(item(head, 1), item(head, 0)) + bias

    def attend(head, weights, inverse):
        output = dot_tn(item(head, 2), weights) * inverse
        turned = turned_ref[pl.ds(head * HD, HD), :].astype(F32)
        stats_ref[8 + head : 9 + head, :] = jnp.sum(output * turned, axis=0, keepdims=True)
        rows_ref[:, pl.ds(head * HD, HD)] = output.T.astype(BF)

    following = score(0)
    earlier = None
    for head in range(HEADS_DEV):
        scores = following
        if head + 1 < HEADS_DEV:
            following = score(head + 1)
        top = jnp.max(scores, axis=0, keepdims=True)
        raised = jnp.exp2((scores - top) * (SCALE * LOG2E))
        inverse = live / jnp.sum(raised, axis=0, keepdims=True)
        weights = raised.astype(BF)
        raised_ref[head] = weights
        stats_ref[head : head + 1, :] = inverse
        if earlier is not None:
            attend(*earlier)
        earlier = (head, weights, inverse)
    attend(*earlier)
    stats_ref[HEADS_DEV:8, :] = jnp.zeros((8 - HEADS_DEV, GROUP), F32)
    stores = []
    for step, ref in ((2, far_ref.at[0]), (3, far_ref.at[1]), (1, near_ref), (0, own_ref)):
        quarter = onehot(iota((ROWS, GROUP), 1) == 4 * iota((ROWS, GROUP), 0) + jnp.bitwise_xor(mine, step))
        piece_ref[step] = dot(quarter, rows_ref[...]).astype(BF)
        store = pltpu.make_async_copy(piece_ref.at[step], ref, piece_sem.at[step])
        store.start()
        stores.append(store)
    inverse_columns = stats_ref[0:8, :].T
    halves = [(head, half) for head in range(HEADS_DEV) for half in range(2)]
    def part_item(head, array, half=None):
        loaders = pl.ds(0, LOADERS) if half is None else pl.ds(half * 64, 64)
        return recv_ref[loaders, :, columns(head, array)].reshape(-1, HD)

    def attended(head, half):
        return dot_nt(part_item(head, 2), grad_ref[pl.ds(half * 256, 256), pl.ds(head * HD, HD)])

    ahead = [attended(*halves[0]), attended(*halves[1])]
    for index, (head, half) in enumerate(halves):
        grad_attend = ahead.pop(0)
        if index + 2 < len(halves):
            ahead.append(attended(*halves[index + 2]))
        rows = slice(half * 256, (half + 1) * 256)
        weights = raised_ref[head, :, rows]
        inverse = stats_ref[head : head + 1, rows]
        row_dot = stats_ref[8 + head : 9 + head, rows]
        grad_scores = (weights.astype(F32) * (grad_attend - row_dot)).astype(BF)
        column = inverse_columns[rows, head : head + 1]
        query = (part_item(head, 0, half).astype(F32) * (column * SCALE)).astype(BF)
        grad = (grad_ref[rows, pl.ds(head * HD, HD)].astype(F32) * column).astype(BF)
        grad_query = (dot_tn(part_item(head, 1), grad_scores) * (inverse * SCALE)).T.astype(BF)
        ret_ref[pl.ds(half * 64, 64), :, columns(head, 0)] = grad_query.reshape(64, 4, HD)
        if half == 0:
            grad_key, grad_value = dot(grad_scores, query), dot(weights, grad)
            continue
        grad_key += dot(grad_scores, query)
        grad_value += dot(weights, grad)
        ret_ref[:, :, columns(head, 1)] = grad_key.astype(BF).reshape(LOADERS, 4, HD)
        ret_ref[:, :, columns(head, 2)] = grad_value.astype(BF).reshape(LOADERS, 4, HD)
        for array in range(3):
            lanes = columns(head, array)
            store = pltpu.make_async_copy(
                ret_ref.at[:, :, lanes], out_ref.at[:, :, lanes], out_sem.at[head, array]
            )
            store.start()
            stores.append(store)
    for store in stores:
        store.wait()


SMEM = pl.BlockSpec(memory_space=pltpu.SMEM)
VMEM = pl.BlockSpec(memory_space=pltpu.VMEM)
HBM = pl.BlockSpec(memory_space=pltpu.HBM)
PARAMS = pltpu.CompilerParams(vmem_limit_bytes=24 * 1024 * 1024)
AHEAD = pl.CostEstimate(flops=15_000_000_000, bytes_accessed=50_000_000, transcendentals=0)
PIECES = jax.ShapeDtypeStruct((2, ROWS, PART), BF)
WHOLE = jax.ShapeDtypeStruct((ROWS, WIDTH), BF)


def in_hbm(array):
    return pltpu.with_memory_space_constraint(array, pltpu.HBM)


def pack(me, table, queries, keys, values, cotangent):
    chunks, far = pl.pallas_call(
        pack_kernel,
        out_shape=(pltpu.HBM((N_DP, N_SP, 4, CHUNK), BF), PIECES),
        in_specs=[SMEM] + [HBM] * 5,
        out_specs=(HBM, VMEM),
        scratch_shapes=[
            pltpu.VMEM((LOADERS, ROWS), jnp.int32),
            pltpu.VMEM((3, ROWS, WIDTH), BF),
            pltpu.VMEM((N_DP, N_SP, 4, CHUNK), BF),
            pltpu.SemaphoreType.DMA,
            pltpu.SemaphoreType.DMA((3,)),
            pltpu.SemaphoreType.DMA((3,)),
            pltpu.SemaphoreType.DMA((2,)),
        ],
        compiler_params=PARAMS,
        name="pack",
    )(me, in_hbm(table), in_hbm(queries), in_hbm(keys), in_hbm(values), in_hbm(cotangent))
    return chunks.reshape(LOADERS, 4, CHUNK), far


def unpack(pick, chunks):
    return pl.pallas_call(
        unpack_kernel,
        out_shape=(pltpu.HBM((ROWS, WIDTH), BF),) * 3,
        in_specs=[VMEM] * 2,
        out_specs=(HBM,) * 3,
        scratch_shapes=[
            pltpu.VMEM((3, ROWS, WIDTH), BF),
            pltpu.SemaphoreType.DMA((3, N_SP)),
        ],
        compiler_params=PARAMS,
        name="unpack",
    )(pick, chunks.reshape(N_DP, N_SP, 4, CHUNK))


def prepare(me, lengths, plan, bins, guide, table, cotangent, pieces):
    return pl.pallas_call(
        prepare_kernel,
        out_shape=(
            jax.ShapeDtypeStruct((GROUP, PART), BF),
            jax.ShapeDtypeStruct((PART, GROUP), BF),
            jax.ShapeDtypeStruct((GROUP, HD), F32),
            jax.ShapeDtypeStruct((8, GROUP), F32),
            jax.ShapeDtypeStruct((ROWS, LOADERS), BF),
        ),
        in_specs=[SMEM] * 5 + [VMEM, HBM] + [VMEM] * 3,
        out_specs=(VMEM,) * 5,
        scratch_shapes=[
            pltpu.VMEM((ROWS, PART), BF),
            pltpu.VMEM((4, ROWS, PART), BF),
            pltpu.VMEM((4, ROWS, PART), BF),
            pltpu.SemaphoreType.DMA,
        ],
        compiler_params=PARAMS,
        cost_estimate=AHEAD,
        name="prepare",
    )(me, lengths, plan, bins, guide, table, in_hbm(cotangent), *pieces)


def collect(me, plan, bins, guide, table, pieces):
    return pl.pallas_call(
        collect_kernel,
        out_shape=WHOLE,
        in_specs=[SMEM] * 4 + [VMEM] * (1 + N_SP),
        out_specs=VMEM,
        compiler_params=PARAMS,
        cost_estimate=AHEAD,
        name="collect",
    )(me, plan, bins, guide, table, *pieces)


def attend(me, bias, live, grad, turned, chunks):
    return pl.pallas_call(
        attend_kernel,
        out_shape=(
            pltpu.HBM((LOADERS, 4, CHUNK), BF),
            pltpu.HBM((ROWS, PART), BF),
            pltpu.HBM((ROWS, PART), BF),
            pltpu.HBM((2, ROWS, PART), BF),
        ),
        in_specs=[SMEM] + [VMEM] * 5,
        out_specs=(HBM,) * 4,
        scratch_shapes=[
            pltpu.VMEM((GROUP, PART), BF),
            pltpu.VMEM((N_SP, ROWS, PART), BF),
            pltpu.VMEM((HEADS_DEV, GROUP, GROUP), BF),
            pltpu.VMEM((16, GROUP), F32),
            pltpu.VMEM((LOADERS, 4, CHUNK), BF),
            pltpu.SemaphoreType.DMA((N_SP,)),
            pltpu.SemaphoreType.DMA((HEADS_DEV, 3)),
        ],
        compiler_params=PARAMS,
        name="attend",
    )(me, bias, live, grad, turned, chunks)


def exchange(chunks):
    return lax.all_to_all(chunks, ("dp", "sp"), split_axis=0, concat_axis=0, tiled=True)


def swap(piece, step):
    return lax.ppermute(piece, "sp", [(i, i ^ step) for i in range(N_SP)])


def swap_pieces(near, far):
    far = swap(far, 2)
    return swap(near, 1), far, swap(far, 1)


def per_device(
    queries,
    key_rows,
    value_rows,
    cotangent,
    lengths,
    sample_plan,
    guide_bins,
    guide_table,
    block_source,
):
    me = (lax.axis_index("dp") * N_SP + lax.axis_index("sp")).astype(jnp.int32).reshape(1)
    table = block_source.reshape(LOADERS, ROWS)
    packed, far = pack(me, table, queries, key_rows, value_rows, cotangent)
    chunks = exchange(packed)
    near = lax.dynamic_slice_in_dim(cotangent, jnp.bitwise_xor(lax.axis_index("sp"), 1) * PART, PART, axis=1)
    grad, turned, bias, live, pick = prepare(
        me, lengths, sample_plan, guide_bins, guide_table, table, cotangent, swap_pieces(near, far)
    )
    grads, own, *outs = attend(me, bias, live, grad, turned, chunks)
    out_pieces = own, *swap_pieces(*outs)
    back = exchange(grads)
    attn_out = collect(me, sample_plan, guide_bins, guide_table, table, out_pieces)
    return attn_out, *unpack(pick, back)


def solution(mesh):
    rows = P(("dp", "sp"), None)
    return jax.shard_map(
        per_device,
        mesh=mesh,
        in_specs=(rows,) * 4 + (P(),) * 5,
        out_specs=(rows,) * 4,
        check_vma=False,
    )
```
